32 devices in a mesh: groups: 2 (over x), ao: 16 (over z, y, core).
Axes of the slice: x: 2, y: 2, z: 4, core: 2. Of those that a mesh axis runs over, the one named last changes fastest.
Arguments:
- b_half: bfloat16 [6144, 8192], P('groups', 'ao'), parts along dimension 0
- significant: int32 [32, 3], P('groups'), parts along dimension 0, may hold values 0 or 1
- live_rows: int32 [32], P('groups'), parts along dimension 0, may hold values from 512 to 3072, as said below
Outputs:
- k_diagonal: float32 [32, 512, 512], P(('groups', 'ao')), parts along dimension 0
- k_upper: float32 [32, 3, 512, 512], P(('groups', 'ao')), parts along dimension 0
- k_lower: float32 [32, 3, 512, 512], P(('groups', 'ao')), parts along dimension 0
The draws below stay inside these ranges and needn't reach their ends.
There are 2 independent parts, one for each index of `groups`. The reference program is written for one: setup_inputs(seed, part) draws one part's arguments, and reference() takes and returns one part's arrays. A program takes and returns all parts, laid end to end along the dimension named above; each array names one. Nothing has to cross between parts.
Inputs may be any that keep to these rules, and one draw needn't show every extreme that they name: `live_rows`: a multiple of 512; every draw has a block with all 3072 rows and one with 512.
All inputs are finite; a program needn't handle non-finite values.
Results may differ from the reference program's by a relative error of at most 0.0003.
Values may be sent and summed in bfloat16 or wider, within the bound.
No kernel may reach another device: no remote copies, remote signals or barrier semaphores. Data moves between devices by JAX's collectives and lax.ppermute only.
A program may use at most 128 MiB of HBM per device.

```python
import jax
import jax.numpy as jnp
from jax import lax

ROWBLK = 512
BS = 512
HOPS = 3
ROWS = 3072
NBLK = 16
NAO = 8192


def draw_b_half(key, part):
    key = jax.random.fold_in(key, 11)
    first, second, third = jax.random.split(key, 3)
    noise = jax.random.normal(first, (ROWS, NAO), jnp.float32)
    shared = jax.random.normal(second, (ROWS, 1), jnp.float32) * jax.random.normal(third, (1, NAO), jnp.float32) * 0.5
    return ((noise + shared) * ROWS ** (-0.375)).astype(jnp.bfloat16)


def draw_live_rows(key, part):
    key = jax.random.fold_in(key, 23)
    first, second, third = jax.random.split(key, 3)
    blocks = ROWS // ROWBLK
    levels = jax.random.randint(first, (NBLK,), 1, blocks + 1)
    topmost = jax.random.randint(second, (), 0, NBLK)
    lowest = (topmost + jax.random.randint(third, (), 1, NBLK)) % NBLK
    levels = levels.at[topmost].set(blocks).at[lowest].set(1)
    return (levels * ROWBLK).astype(jnp.int32)


def touch_ends(drawn, rng, low, top_value):
    longest = drawn.shape.index(max(drawn.shape))
    spots = []
    for shift in (0, 1):
        where = [jax.random.randint(jax.random.fold_in(rng, axis), (), 0, length) for axis, length in enumerate(drawn.shape)]
        where[longest] = (where[longest] + shift) % drawn.shape[longest]
        spots.append(tuple(where))
    return drawn.at[spots[0]].set(low).at[spots[1]].set(top_value)


def setup_inputs(seed: int = 0, part: int = 0) -> dict:
    streams_of = jax.random.split(jax.random.key(seed), 4)
    own_keys = jax.random.split(jax.random.fold_in(streams_of[3], part), 4)
    b_half = draw_b_half(jax.random.fold_in(jax.random.fold_in(streams_of[3], part), 71), part)
    significant = touch_ends((jax.random.randint(own_keys[1], (NBLK, HOPS), 0, 4) < 3).astype(jnp.int32), jax.random.fold_in(own_keys[1], 1), 0, 1)
    live_rows = draw_live_rows(jax.random.fold_in(jax.random.fold_in(streams_of[3], part), 71), part)
    return {"b_half": b_half, "significant": significant, "live_rows": live_rows}


def pair_tile(first_block, second_block, row_limit):
    row_ids = jnp.arange(ROWS, dtype=jnp.int32)[:, None]
    masked = jnp.where(row_ids < row_limit, first_block, jnp.zeros_like(first_block))
    return jnp.dot(masked.T, second_block, preferred_element_type=jnp.float32)


def reference(b_half, significant, live_rows):
    def one_block(position):
        own_block = lax.dynamic_slice_in_dim(b_half, (position * BS).astype(jnp.int32), BS, 1)
        own_count = live_rows[position]
        diagonal = pair_tile(own_block, own_block, own_count)
        uppers = []
        lowers = []
        for offset in range(HOPS):
            upper_id = position + offset + 1
            clamped = jnp.minimum(upper_id, NBLK - 1).astype(jnp.int32)
            partner = lax.dynamic_slice_in_dim(b_half, (clamped * BS).astype(jnp.int32), BS, 1)
            wanted = (upper_id < NBLK) & (significant[clamped * 0 + position, offset] == 1)
            limit_up = jnp.where(wanted, jnp.minimum(own_count, live_rows[clamped]), 0)
            uppers.append(pair_tile(own_block, partner, limit_up))
            lower_id = position - offset - 1
            lowest = jnp.maximum(lower_id, 0).astype(jnp.int32)
            partner_low = lax.dynamic_slice_in_dim(b_half, (lowest * BS).astype(jnp.int32), BS, 1)
            wanted_low = (lower_id >= 0) & (significant[lowest, offset] == 1)
            limit_low = jnp.where(wanted_low, jnp.minimum(own_count, live_rows[lowest]), 0)
            lowers.append(pair_tile(own_block, partner_low, limit_low))
        return diagonal, jnp.stack(uppers), jnp.stack(lowers)

    k_diagonal, k_upper, k_lower = lax.map(one_block, jnp.arange(NBLK, dtype=jnp.int32))
    return k_diagonal, k_upper, k_lower
```

```python
import functools

import jax
import jax.numpy as jnp
from jax import lax
from jax.experimental import pallas as pl
from jax.experimental.pallas import tpu as pltpu
from jax.sharding import PartitionSpec as P

ROWBLK = 512
HOPS = 3
LEVEL = 4
SPLIT = 3
DIRECT = 1


def level_route(block_total, moves):
    levels = block_total // LEVEL
    return [
        (LEVEL * z + place, LEVEL * (z + step) + new)
        for z in range(levels)
        for place, step, new in moves
        if 0 <= z + step < levels
    ]


def tiles_kernel(position_ref, live_ref, sig_ref, *refs, pieces, block_total):
    own_ref = refs[0]
    partner_refs = refs[1 : 1 + 6 * pieces]
    diag_ref, up_ref, low_ref = refs[1 + 6 * pieces : 4 + 6 * pieces]
    own, own_t, held, tile, own_sem, in_sem, out_sem = refs[4 + 6 * pieces :]
    steps = own.shape[0]
    per_piece = steps // pieces
    position = position_ref[0]
    place = lax.rem(position, LEVEL)
    own_count = live_ref[position] // ROWBLK

    upward = place >= 2
    edge = (place == 0) | (place == 3)
    d_core = jnp.where(lax.rem(place, 2) == 0, 1, -1)
    d_y = jnp.where(place < 2, 2, -2)
    d_both = (LEVEL - 1) - 2 * place
    d_far = jnp.where(lax.rem(place, 2) == 0, -3, 3)
    d_relay = jnp.where(upward, 2, -2)
    d_last = jnp.where(edge, jnp.where(upward, 1, -1), jnp.where(upward, 3, -3))
    dists = [d_core, d_y, d_both, d_far, d_relay, d_last]

    def count_of(dist):
        other = position + dist
        inside = (other >= 0) & (other < block_total)
        safe = jnp.clip(other, 0, block_total - 1)
        first = jnp.minimum(position, safe)
        hop = jnp.clip(jnp.abs(dist) - 1, 0, HOPS - 1)
        rows = jnp.minimum(own_count, live_ref[safe] // ROWBLK)
        return jnp.where(inside, rows * sig_ref[first, hop], 0)

    counts = [count_of(d) for d in dists]

    def own_copy(r):
        return pltpu.make_async_copy(own_ref.at[pl.ds(r * ROWBLK, ROWBLK)], own.at[r], own_sem.at[r])

    def held_copy(p, r):
        source = partner_refs[p * pieces + r // per_piece]
        return pltpu.make_async_copy(
            source.at[pl.ds((r % per_piece) * ROWBLK, ROWBLK)], held.at[p % 2, r], in_sem.at[p % 2, r]
        )

    def start_partner(p):
        for r in range(steps):
            @pl.when(r < counts[p])
            def _():
                held_copy(p, r).start()

    def wait_partner(p):
        for r in range(steps):
            @pl.when(r < counts[p])
            def _():
                held_copy(p, r).wait()

    for r in range(steps):
        @pl.when(r < own_count)
        def _():
            own_copy(r).start()
    start_partner(0)
    for r in range(steps):
        @pl.when(r < own_count)
        def _():
            own_copy(r).wait()

    def turn(r, _):
        own_t[r] = own[r].T
        return 0

    lax.fori_loop(0, own_count, turn, 0)

    def make_tile(slot, count, load):
        tile[slot] = jnp.zeros(tile.shape[1:], jnp.float32)

        def add(r, _):
            tile[slot] += jnp.dot(own_t[r], load(r), preferred_element_type=jnp.float32)
            return 0

        lax.fori_loop(0, count, add, 0)

    make_tile(0, own_count, lambda r: own[r])
    pltpu.make_async_copy(tile.at[0], diag_ref.at[0], out_sem.at[0]).start()

    def wait_tile(slot):
        pltpu.make_async_copy(tile.at[slot], diag_ref.at[0], out_sem.at[slot]).wait()

    for p in range(6):
        slot = (p + 1) % 2
        if p < 5:
            start_partner(p + 1)
        wait_partner(p)
        if p >= 1:
            wait_tile(slot)
        make_tile(slot, counts[p], lambda r: held[p % 2, r])
        hop = jnp.clip(jnp.abs(dists[p]) - 1, 0, HOPS - 1)

        @pl.when(dists[p] > 0)
        def _():
            pltpu.make_async_copy(tile.at[slot], up_ref.at[0, hop], out_sem.at[slot]).start()

        @pl.when(dists[p] < 0)
        def _():
            pltpu.make_async_copy(tile.at[slot], low_ref.at[0, hop], out_sem.at[slot]).start()

    wait_tile(1)
    wait_tile(0)


def make_tiles(position, live_rows, significant, own, partners, block_total):
    rows, cols = own.shape
    steps = rows // ROWBLK
    pieces = len(partners[0])
    flat = [piece for partner in partners for piece in partner]
    smem = pl.BlockSpec(memory_space=pltpu.SMEM)
    hbm = pl.BlockSpec(memory_space=pl.ANY)
    return pl.pallas_call(
        functools.partial(tiles_kernel, pieces=pieces, block_total=block_total),
        out_shape=(
            jax.ShapeDtypeStruct((1, cols, cols), jnp.float32),
            jax.ShapeDtypeStruct((1, HOPS, cols, cols), jnp.float32),
            jax.ShapeDtypeStruct((1, HOPS, cols, cols), jnp.float32),
        ),
        in_specs=[smem] * 3 + [hbm] * (1 + len(flat)),
        out_specs=(hbm,) * 3,
        scratch_shapes=[
            pltpu.VMEM((steps, ROWBLK, cols), own.dtype),
            pltpu.VMEM((steps, cols, ROWBLK), own.dtype),
            pltpu.VMEM((2, steps, ROWBLK, cols), own.dtype),
            pltpu.VMEM((2, cols, cols), jnp.float32),
            pltpu.SemaphoreType.DMA((steps,)),
            pltpu.SemaphoreType.DMA((2, steps)),
            pltpu.SemaphoreType.DMA((2,)),
        ],
        compiler_params=pltpu.CompilerParams(vmem_limit_bytes=40 * 2**20),
    )(position, live_rows, significant, own, *flat)


def per_device(b_half, significant, live_rows):
    block_total = lax.axis_size("ao")
    position = lax.axis_index("ao").astype(jnp.int32)
    piece_rows = b_half.shape[0] // SPLIT
    own = [b_half[i * piece_rows : (i + 1) * piece_rows] for i in range(SPLIT)]

    def send(block, moves):
        return lax.ppermute(block, "ao", level_route(block_total, moves))

    cores = [(j, 0, j ^ 1) for j in range(LEVEL)]
    across = [(j, 0, j ^ 2) for j in range(LEVEL)]
    far = [(1, 1, 0), (0, -1, 1), (3, 1, 2), (2, -1, 3)]
    relay = [(0, 1, 0), (1, 1, 1), (2, -1, 2), (3, -1, 3)]
    relay_edges = [(0, 1, 0), (3, -1, 3)]
    far_across = [(2, 0, 0), (1, 0, 3)]
    edges_in = [(0, 0, 1), (3, 0, 2)]

    y_part, both_part, relay_part, last_part = [], [], [], []
    far_part = [send(own[i], far) for i in reversed(range(SPLIT))][::-1]
    core_part = [send(own[i], cores) for i in range(SPLIT)]
    on_inner = (position % LEVEL == 1) | (position % LEVEL == 2)
    for i in range(SPLIT):
        y_part.append(send(own[i], across))
        both_part.append(send(y_part[i], cores))
        if i < SPLIT - DIRECT:
            relay_part.append(send(y_part[i], relay))
            last_part.append(send(relay_part[i], cores))
        else:
            second = send(y_part[i], relay_edges)
            first = send(far_part[i], far_across)
            inner_last = send(second, edges_in)
            inner_relay = send(first, edges_in)
            relay_part.append(jnp.where(on_inner, inner_relay, second))
            last_part.append(jnp.where(on_inner, inner_last, first))
    return make_tiles(
        position[None],
        live_rows,
        significant,
        b_half,
        [core_part, y_part, both_part, far_part, relay_part, last_part],
        block_total,
    )


def solution(mesh):
    in_specs = (P("groups", "ao"), P("groups", None), P("groups"))
    out_specs = (
        P(("groups", "ao"), None, None),
        P(("groups", "ao"), None, None, None),
        P(("groups", "ao"), None, None, None),
    )
    return jax.shard_map(
        per_device, mesh=mesh, in_specs=in_specs, out_specs=out_specs, check_vma=False
    )
```

```python
import functools

import jax
import jax.numpy as jnp
from jax import lax
from jax.experimental import pallas as pl
from jax.experimental.pallas import tpu as pltpu
from jax.sharding import PartitionSpec as P

ROWBLK = 512
HOPS = 3
VMEM_LIMIT = 63 * 2**20
LEVEL = 4
HEAD = 3
TURNS = (2, 1)

SMEM = pl.BlockSpec(memory_space=pltpu.SMEM)
HBM = pl.BlockSpec(memory_space=pltpu.HBM)


def level_route(block_total, moves):
    levels = block_total // LEVEL
    return [
        (LEVEL * z + place, LEVEL * (z + step) + new)
        for z in range(levels)
        for place, step, new in moves
        if 0 <= z + step < levels
    ]


class Geometry:
    def __init__(self, position_ref, live_ref, sig_ref, block_total):
        self.live_ref, self.sig_ref, self.block_total = live_ref, sig_ref, block_total
        self.me = position_ref[0]
        self.place = lax.rem(self.me, LEVEL)
        even = lax.rem(self.place, 2) == 0
        self.upper = self.place >= 2
        self.edge = (self.place == 0) | (self.place == 3)
        self.core = self.me + jnp.where(even, 1, -1)
        self.across = self.me + jnp.where(self.upper, -2, 2)
        self.far = self.me + jnp.where(even, -3, 3)
        self.relay = self.me + jnp.where(self.upper, 2, -2)
        self.both = self.me + (LEVEL - 1) - 2 * self.place
        self.last = self.me + jnp.where(self.edge, 1, 3) * jnp.where(self.upper, 1, -1)

    def live(self, block):
        return self.live_ref[jnp.clip(block, 0, self.block_total - 1)] // ROWBLK

    def count(self, first, second):
        low = jnp.clip(jnp.minimum(first, second), 0, self.block_total - 1)
        hop = jnp.clip(jnp.abs(first - second) - 1, 0, HOPS - 1)
        inside = (second >= 0) & (second < self.block_total)
        rows = jnp.minimum(self.live(first), self.live(second))
        return jnp.where(inside, rows * self.sig_ref[low, hop], 0)

    def place_tile(self, tile, other, up_ref, low_ref, sem, enable=True):
        dist = other - self.me
        hop = jnp.clip(jnp.abs(dist) - 1, 0, HOPS - 1)

        @pl.when(enable & (dist > 0))
        def _():
            pltpu.make_async_copy(tile, up_ref.at[0, hop], sem).start()

        @pl.when(enable & (dist < 0))
        def _():
            pltpu.make_async_copy(tile, low_ref.at[0, hop], sem).start()

    def wait_tile(self, tile, up_ref, sem):
        pltpu.make_async_copy(tile, up_ref.at[0, 0], sem).wait()


def rows_at(ref, r):
    return ref.at[pl.ds(r * ROWBLK, ROWBLK)]


def dot_into(total, left, right):
    total[...] += jnp.dot(left, right, preferred_element_type=jnp.float32)


def gate_kernel(*refs):
    del refs


def after(array, *tokens):
    return pl.pallas_call(
        gate_kernel,
        out_shape=jax.ShapeDtypeStruct(array.shape, array.dtype),
        in_specs=[HBM] * (1 + len(tokens)),
        out_specs=HBM,
        input_output_aliases={0: 0},
        compiler_params=pltpu.CompilerParams(vmem_limit_bytes=VMEM_LIMIT),
    )(array, *tokens)


def pick_kernel(position_ref, edge_ref, inner_ref, *refs, low, sizes):
    outs, (held, in_sem, out_sem) = refs[: len(sizes)], refs[len(sizes) :]
    place = lax.rem(position_ref[0], LEVEL)
    inner = (place == 1) | (place == 2)
    places = [(out, k) for out, size in zip(outs, sizes) for k in range(size)]
    copies = []
    for k, (out, at) in enumerate(places):
        pl.when(inner)(pltpu.make_async_copy(rows_at(inner_ref, low + k), held.at[k], in_sem.at[k]).start)
        pl.when(jnp.logical_not(inner))(pltpu.make_async_copy(rows_at(edge_ref, k), held.at[k], in_sem.at[k]).start)
        copies.append(pltpu.make_async_copy(held.at[k], rows_at(out, at), out_sem.at[k]))
    for k, copy in enumerate(copies):
        pltpu.make_async_copy(rows_at(edge_ref, k), held.at[k], in_sem.at[k]).wait()
        copy.start()
    for copy in copies:
        copy.wait()


def pick(position, edge, inner, low, sizes, *tokens):
    rows, cols = edge.shape
    total = rows // ROWBLK

    def body(position_ref, edge_ref, inner_ref, *refs):
        pick_kernel(position_ref, edge_ref, inner_ref, *refs[len(tokens) :], low=low, sizes=sizes)

    return pl.pallas_call(
        body,
        out_shape=tuple(jax.ShapeDtypeStruct((size * ROWBLK, cols), edge.dtype) for size in sizes),
        in_specs=[SMEM] + [HBM] * (2 + len(tokens)),
        out_specs=(HBM,) * len(sizes),
        scratch_shapes=[
            pltpu.VMEM((total, ROWBLK, cols), edge.dtype),
            pltpu.SemaphoreType.DMA((total,)),
            pltpu.SemaphoreType.DMA((total,)),
        ],
        compiler_params=pltpu.CompilerParams(vmem_limit_bytes=VMEM_LIMIT),
    )(position, edge, inner, *tokens)


def own_kernel(position_ref, live_ref, sig_ref, own_ref, diag_ref, own_t_ref, own, own_t, tile, in_sem, turned_sem, out_sem, *, block_total):
    steps = own.shape[0]
    geo = Geometry(position_ref, live_ref, sig_ref, block_total)
    count = geo.live(geo.me)

    def in_copy(r):
        return pltpu.make_async_copy(rows_at(own_ref, r), own.at[r], in_sem.at[r])

    def turned_copy(r):
        return pltpu.make_async_copy(own_t.at[r], own_t_ref.at[r], turned_sem.at[r])

    for r in range(steps):
        pl.when(r < count)(in_copy(r).start)
    tile[...] = jnp.zeros_like(tile)

    @pl.loop(0, count)
    def _(r):
        in_copy(r).wait()
        own_t[r] = own[r].T
        turned_copy(r).start()
        dot_into(tile, own_t[r], own[r])

    out_copy = pltpu.make_async_copy(tile, diag_ref.at[0], out_sem.at[0])
    out_copy.start()

    @pl.loop(0, count)
    def _(r):
        turned_copy(r).wait()

    out_copy.wait()


def own_tile(scalars, own, block_total):
    rows, cols = own.shape
    steps = rows // ROWBLK
    return pl.pallas_call(
        functools.partial(own_kernel, block_total=block_total),
        out_shape=(
            jax.ShapeDtypeStruct((1, cols, cols), jnp.float32),
            jax.ShapeDtypeStruct((steps, cols, ROWBLK), own.dtype),
        ),
        in_specs=[SMEM] * 3 + [HBM],
        out_specs=(HBM,) * 2,
        scratch_shapes=[
            pltpu.VMEM((steps, ROWBLK, cols), own.dtype),
            pltpu.VMEM((steps, cols, ROWBLK), own.dtype),
            pltpu.VMEM((cols, cols), jnp.float32),
            pltpu.SemaphoreType.DMA((steps,)),
            pltpu.SemaphoreType.DMA((steps,)),
            pltpu.SemaphoreType.DMA((1,)),
        ],
        compiler_params=pltpu.CompilerParams(vmem_limit_bytes=VMEM_LIMIT),
        cost_estimate=pl.CostEstimate(
            flops=2 * rows * cols * cols, bytes_accessed=4 * rows * cols + 4 * cols * cols, transcendentals=0
        ),
    )(*scalars, own)


def core_kernel(
    position_ref, live_ref, sig_ref, core_ref, own_t_ref, up_ref, low_ref, core_t_ref, own_t, core, core_t, tile, sems,
    turned_sem, out_sem, *, block_total,
):
    steps = core.shape[0]
    geo = Geometry(position_ref, live_ref, sig_ref, block_total)
    core_count = geo.live(geo.core)
    pair_count = geo.count(geo.me, geo.core)

    def core_copy(r):
        return pltpu.make_async_copy(rows_at(core_ref, r), core.at[r], sems.at[0, r])

    def own_copy(r):
        return pltpu.make_async_copy(own_t_ref.at[r], own_t.at[r], sems.at[1, r])

    def turned_copy(r):
        return pltpu.make_async_copy(core_t.at[r], core_t_ref.at[r], turned_sem.at[r])

    for r in range(steps):
        pl.when(r < core_count)(core_copy(r).start)
        pl.when(r < pair_count)(own_copy(r).start)
    tile[...] = jnp.zeros_like(tile)

    @pl.loop(0, core_count)
    def _(r):
        core_copy(r).wait()
        core_t[r] = core[r].T
        turned_copy(r).start()

        @pl.when(r < pair_count)
        def _():
            own_copy(r).wait()
            dot_into(tile, own_t[r], core[r])

    geo.place_tile(tile, geo.core, up_ref, low_ref, out_sem.at[0])

    @pl.loop(0, core_count)
    def _(r):
        turned_copy(r).wait()

    geo.wait_tile(tile, up_ref, out_sem.at[0])


def core_tile(scalars, core, own_t, block_total):
    rows, cols = core.shape
    steps = rows // ROWBLK
    three = jax.ShapeDtypeStruct((1, HOPS, cols, cols), jnp.float32)
    return pl.pallas_call(
        functools.partial(core_kernel, block_total=block_total),
        out_shape=(three, three, jax.ShapeDtypeStruct(own_t.shape, own_t.dtype)),
        in_specs=[SMEM] * 3 + [HBM] * 2,
        out_specs=(HBM,) * 3,
        scratch_shapes=[
            pltpu.VMEM((steps, cols, ROWBLK), core.dtype),
            pltpu.VMEM((steps, ROWBLK, cols), core.dtype),
            pltpu.VMEM((steps, cols, ROWBLK), core.dtype),
            pltpu.VMEM((cols, cols), jnp.float32),
            pltpu.SemaphoreType.DMA((2, steps)),
            pltpu.SemaphoreType.DMA((steps,)),
            pltpu.SemaphoreType.DMA((1,)),
        ],
        compiler_params=pltpu.CompilerParams(vmem_limit_bytes=VMEM_LIMIT),
        cost_estimate=pl.CostEstimate(
            flops=2 * rows * cols * cols, bytes_accessed=6 * rows * cols + 4 * cols * cols, transcendentals=0
        ),
    )(*scalars, core, own_t)


def pair_kernel(
    position_ref, live_ref, sig_ref, own_t_ref, core_t_ref, piece_refs, before, outs, own_t, core_t, held, tiles, sems,
    before_sem, out_sem, *, which, low, high, sources, final, block_total,
):
    geo = Geometry(position_ref, live_ref, sig_ref, block_total)
    other = getattr(geo, which)
    shared = which != "far"
    count = geo.count(geo.me, other)
    core_count = geo.count(geo.core, other) if shared else 0
    either = jnp.maximum(count, core_count)

    for r in range(low, high):
        at, (ref, offset) = r - low, sources[r]
        own_copy = pltpu.make_async_copy(own_t_ref.at[r], own_t.at[at], sems.at[0, at])
        pl.when(r < count)(own_copy.start)
        if shared:
            core_copy = pltpu.make_async_copy(core_t_ref.at[r], core_t.at[at], sems.at[1, at])
            pl.when(r < core_count)(core_copy.start)
        held_copy = pltpu.make_async_copy(rows_at(piece_refs[ref], offset), held.at[at], sems.at[2, at])
        pl.when(r < either)(held_copy.start)

    if before:
        loads = [pltpu.make_async_copy(before[i], tiles.at[i], before_sem.at[i]) for i in range(2)]
        for load in loads:
            load.start()
        for load in loads:
            load.wait()
    else:
        tiles[...] = jnp.zeros_like(tiles)

    @pl.loop(0, high - low)
    def _(at):
        r = at + low

        @pl.when(r < either)
        def _():
            pltpu.make_async_copy(rows_at(piece_refs[0], 0), held.at[at], sems.at[2, at]).wait()

        @pl.when(r < count)
        def _():
            pltpu.make_async_copy(own_t_ref.at[0], own_t.at[at], sems.at[0, at]).wait()
            dot_into(tiles.at[0], own_t[at], held[at])

        if shared:
            @pl.when(r < core_count)
            def _():
                pltpu.make_async_copy(core_t_ref.at[0], core_t.at[at], sems.at[1, at]).wait()
                dot_into(tiles.at[1], core_t[at], held[at])

    if shared:
        swap_copy = pltpu.make_async_copy(tiles.at[1], outs[-1], out_sem.at[1])
        swap_copy.start()
    if final:
        geo.place_tile(tiles.at[0], other, outs[0], outs[1], out_sem.at[0])
        geo.wait_tile(tiles.at[0], outs[0], out_sem.at[0])
    else:
        own_out = pltpu.make_async_copy(tiles.at[0], outs[0], out_sem.at[0])
        own_out.start()
        own_out.wait()
    if shared:
        swap_copy.wait()


def pair_tiles(scalars, turned, which, pieces, low, high, before, outputs, block_total):
    steps, cols, _ = turned[0].shape
    tile = jax.ShapeDtypeStruct((cols, cols), jnp.float32)
    final = outputs is not None
    places = [(i, k) for i, piece in enumerate(pieces) for k in range(piece.shape[0] // ROWBLK)]
    sources = dict(zip(range(low, high), places))
    before, chained = list(before or ()), list(outputs or ())
    n_in, n_before = len(pieces), len(before)
    n_out = (2 if final else 1) + (which != "far")

    def body(position_ref, live_ref, sig_ref, own_t_ref, core_t_ref, *refs):
        outs_at = n_in + n_before + len(chained)
        pair_kernel(
            position_ref, live_ref, sig_ref, own_t_ref, core_t_ref, refs[:n_in], refs[n_in : n_in + n_before],
            refs[outs_at : outs_at + n_out], *refs[outs_at + n_out :],
            which=which, low=low, high=high, sources=sources, final=final, block_total=block_total,
        )

    span = high - low
    return pl.pallas_call(
        body,
        out_shape=tuple(jax.ShapeDtypeStruct(c.shape, c.dtype) for c in chained) + (tile,) * (n_out - len(chained)),
        in_specs=[SMEM] * 3 + [HBM] * (2 + n_in + n_before + len(chained)),
        out_specs=(HBM,) * n_out,
        scratch_shapes=[pltpu.VMEM((span, cols, ROWBLK), turned[0].dtype)] * 2
        + [
            pltpu.VMEM((span, ROWBLK, cols), turned[0].dtype),
            pltpu.VMEM((2, cols, cols), jnp.float32),
            pltpu.SemaphoreType.DMA((3, span)),
            pltpu.SemaphoreType.DMA((2,)),
            pltpu.SemaphoreType.DMA((2,)),
        ],
        input_output_aliases={5 + n_in + n_before + i: i for i in range(len(chained))},
        compiler_params=pltpu.CompilerParams(vmem_limit_bytes=VMEM_LIMIT),
        cost_estimate=pl.CostEstimate(
            flops=4 * span * ROWBLK * cols * cols,
            bytes_accessed=6 * span * ROWBLK * cols + 16 * cols * cols,
            transcendentals=0,
        ),
    )(*scalars, *turned, *pieces, *before, *chained)


def place_kernel(position_ref, live_ref, sig_ref, tile_ref, _up, _low, up_ref, low_ref, tile, in_sem, out_sem, *, block_total):
    geo = Geometry(position_ref, live_ref, sig_ref, block_total)
    copy = pltpu.make_async_copy(tile_ref, tile, in_sem.at[0])
    copy.start()
    copy.wait()
    geo.place_tile(tile, geo.both, up_ref, low_ref, out_sem.at[0])
    geo.wait_tile(tile, up_ref, out_sem.at[0])


def place_both(scalars, tile, outputs, block_total):
    return pl.pallas_call(
        functools.partial(place_kernel, block_total=block_total),
        out_shape=tuple(jax.ShapeDtypeStruct(o.shape, o.dtype) for o in outputs),
        in_specs=[SMEM] * 3 + [HBM] * 3,
        out_specs=(HBM,) * 2,
        scratch_shapes=[
            pltpu.VMEM(tile.shape, jnp.float32),
            pltpu.SemaphoreType.DMA((1,)),
            pltpu.SemaphoreType.DMA((1,)),
        ],
        input_output_aliases={4: 0, 5: 1},
        compiler_params=pltpu.CompilerParams(vmem_limit_bytes=VMEM_LIMIT),
    )(*scalars, tile, *outputs)


def end_kernel(
    position_ref, live_ref, sig_ref, own_t_ref, piece_refs, before, outs, own_t, held, tiles, sems, own_sem, before_sem,
    out_sem, *, low, sources, block_total,
):
    span = own_t.shape[0]
    geo = Geometry(position_ref, live_ref, sig_ref, block_total)
    others = (geo.relay, geo.last)
    counts = [geo.count(geo.me, other) for other in others]
    either = jnp.maximum(*counts)

    def own_copy(at):
        return pltpu.make_async_copy(own_t_ref.at[low + at], own_t.at[at], own_sem.at[at])

    loads = [pltpu.make_async_copy(before[i], tiles.at[i], before_sem.at[i]) for i in range(2)]
    for at in range(span):
        pl.when(low + at < either)(own_copy(at).start)
    for i in range(2):
        loads[i].start()
        for at in range(span):
            ref, offset = sources[i][at]
            held_copy = pltpu.make_async_copy(rows_at(piece_refs[ref], offset), held.at[i, at], sems.at[i, at])
            pl.when(low + at < counts[i])(held_copy.start)
    for at in range(span):
        pl.when(low + at < either)(own_copy(at).wait)
    for i in range(2):
        loads[i].wait()

        @pl.loop(0, jnp.maximum(counts[i] - low, 0))
        def _(at):
            pltpu.make_async_copy(rows_at(piece_refs[0], 0), held.at[i, at], sems.at[i, at]).wait()
            dot_into(tiles.at[i], own_t[at], held[i, at])

        geo.place_tile(tiles.at[i], others[i], outs[0], outs[1], out_sem.at[i])
    for i in range(2):
        geo.wait_tile(tiles.at[i], outs[0], out_sem.at[i])


def end_tiles(scalars, own_t, pieces, swapped, low, before, outputs, block_total):
    steps, cols, _ = own_t.shape
    span = steps - low
    arrays = [*pieces, *swapped]
    sources = [
        [(i + first, k) for i, piece in enumerate(group) for k in range(piece.shape[0] // ROWBLK)]
        for first, group in ((0, pieces), (len(pieces), swapped))
    ]
    n_in = len(arrays)

    def body(position_ref, live_ref, sig_ref, own_t_ref, *refs):
        end_kernel(
            position_ref, live_ref, sig_ref, own_t_ref, refs[:n_in], refs[n_in : n_in + 2], refs[n_in + 4 : n_in + 6],
            *refs[n_in + 6 :], low=low, sources=sources, block_total=block_total,
        )

    return pl.pallas_call(
        body,
        out_shape=tuple(jax.ShapeDtypeStruct(o.shape, o.dtype) for o in outputs),
        in_specs=[SMEM] * 3 + [HBM] * (5 + n_in),
        out_specs=(HBM,) * 2,
        scratch_shapes=[
            pltpu.VMEM((span, cols, ROWBLK), own_t.dtype),
            pltpu.VMEM((2, span, ROWBLK, cols), own_t.dtype),
            pltpu.VMEM((2, cols, cols), jnp.float32),
            pltpu.SemaphoreType.DMA((2, span)),
            pltpu.SemaphoreType.DMA((span,)),
            pltpu.SemaphoreType.DMA((2,)),
            pltpu.SemaphoreType.DMA((2,)),
        ],
        input_output_aliases={6 + n_in: 0, 7 + n_in: 1},
        compiler_params=pltpu.CompilerParams(vmem_limit_bytes=VMEM_LIMIT),
    )(*scalars, own_t, *arrays, *before, *outputs)


def per_device(b_half, significant, live_rows):
    block_total = lax.axis_size("ao")
    position = lax.axis_index("ao").astype(jnp.int32)[None]
    scalars = (position, live_rows, significant)
    steps = b_half.shape[0] // ROWBLK

    def send(block, moves):
        return lax.ppermute(block, "ao", level_route(block_total, moves))

    cores = [(j, 0, j ^ 1) for j in range(LEVEL)]
    across = [(j, 0, j ^ 2) for j in range(LEVEL)]
    far = [(1, 1, 0), (0, -1, 1), (3, 1, 2), (2, -1, 3)]
    relay = [(0, 1, 0), (1, 1, 1), (2, -1, 2), (3, -1, 3)]
    turn = [(0, 1, 0), (3, -1, 3), (1, 0, 2), (2, 0, 1)]

    y_head = send(b_half[: HEAD * ROWBLK], across)
    y_tail = send(b_half[HEAD * ROWBLK :], across)
    core = send(b_half, cores)
    far_block = send(b_half, far)

    diagonal, own_t = own_tile(scalars, b_half, block_total)
    upper, lower, core_t = core_tile(scalars, core, own_t, block_total)
    turned = (own_t, core_t)
    y_head = after(y_head, core_t)
    relayed = send(y_head, relay)
    upper, lower = pair_tiles(scalars, turned, "far", [far_block], 0, steps, None, (upper, lower), block_total)
    y_partial = pair_tiles(scalars, turned, "across", [y_head], 0, HEAD, None, None, block_total)

    turns = [send(piece, turn) for piece in pick(position, y_tail, far_block, HEAD, TURNS, upper, y_partial[0])]
    own_part, core_part = pair_tiles(scalars, turned, "relay", [relayed], 0, HEAD, None, None, block_total)
    upper, lower, both = pair_tiles(
        scalars, turned, "across", [y_tail], HEAD, steps, y_partial, (upper, lower), block_total
    )
    upper, lower = place_both(scalars, send(both, cores), (upper, lower), block_total)
    swapped = [send(piece, cores) for piece in turns]
    upper, lower = end_tiles(
        scalars, own_t, turns, swapped, HEAD, (own_part, send(core_part, cores)), (upper, lower), block_total
    )
    return diagonal, upper, lower


def solution(mesh):
    in_specs = (P("groups", "ao"), P("groups", None), P("groups"))
    out_specs = (
        P(("groups", "ao"), None, None),
        P(("groups", "ao"), None, None, None),
        P(("groups", "ao"), None, None, None),
    )
    return jax.shard_map(
        per_device, mesh=mesh, in_specs=in_specs, out_specs=out_specs, check_vma=False
    )
```

```python
import functools

import jax
import jax.numpy as jnp
from jax import lax
from jax.experimental import pallas as pl
from jax.experimental.pallas import tpu as pltpu
from jax.sharding import PartitionSpec as P

ROWBLK = 512
HOPS = 3
VMEM_LIMIT = 28 * 2**20
VMEM_ALL = 63 * 2**20
LEVEL = 4
PARTS = 4
TURNS = (2, 1)
HEAD = 3

SMEM = pl.BlockSpec(memory_space=pltpu.SMEM)
HBM = pl.BlockSpec(memory_space=pltpu.HBM)
ANY = pl.BlockSpec(memory_space=pl.ANY)
TOKEN = jax.ShapeDtypeStruct((8, 128), jnp.float32)


def level_route(block_total, moves):
    levels = block_total // LEVEL
    return [
        (LEVEL * z + place, LEVEL * (z + step) + new)
        for z in range(levels)
        for place, step, new in moves
        if 0 <= z + step < levels
    ]


def start_tile(source, target, sem):
    rows = source.shape[0] // PARTS
    for part in range(PARTS):
        at = pl.ds(part * rows, rows)
        pltpu.make_async_copy(source.at[at], target.at[at], sem).start()


def wait_tile(tile, sem):
    pltpu.make_async_copy(tile, tile, sem).wait()


class Geometry:
    def __init__(self, position_ref, live_ref, sig_ref, block_total):
        self.live_ref, self.sig_ref, self.block_total = live_ref, sig_ref, block_total
        self.me = position_ref[0]
        self.place = lax.rem(self.me, LEVEL)
        even = lax.rem(self.place, 2) == 0
        self.upper = self.place >= 2
        self.edge = (self.place == 0) | (self.place == 3)
        self.core = self.me + jnp.where(even, 1, -1)
        self.across = self.me + jnp.where(self.upper, -2, 2)
        self.far = self.me + jnp.where(even, -3, 3)
        self.relay = self.me + jnp.where(self.upper, 2, -2)
        self.both = self.me + (LEVEL - 1) - 2 * self.place
        self.last = self.me + jnp.where(self.edge, 1, 3) * jnp.where(self.upper, 1, -1)

    def live(self, block):
        return self.live_ref[jnp.clip(block, 0, self.block_total - 1)] // ROWBLK

    def count(self, first, second):
        low = jnp.clip(jnp.minimum(first, second), 0, self.block_total - 1)
        hop = jnp.clip(jnp.abs(first - second) - 1, 0, HOPS - 1)
        inside = (second >= 0) & (second < self.block_total)
        rows = jnp.minimum(self.live(first), self.live(second))
        return jnp.where(inside, rows * self.sig_ref[low, hop], 0)

    def place_tile(self, tile, other, up_ref, low_ref, sem, enable=True):
        dist = other - self.me
        hop = jnp.clip(jnp.abs(dist) - 1, 0, HOPS - 1)

        @pl.when(enable & (dist > 0))
        def _():
            start_tile(tile, up_ref.at[0, hop], sem)

        @pl.when(enable & (dist < 0))
        def _():
            start_tile(tile, low_ref.at[0, hop], sem)


def rows_at(ref, r):
    return ref.at[pl.ds(r * ROWBLK, ROWBLK)]


def dot_into(total, left, right):
    total[...] += jnp.dot(left, right, preferred_element_type=jnp.float32)


def gate_kernel(*refs):
    del refs


def after(array, *tokens):
    return pl.pallas_call(
        gate_kernel,
        out_shape=jax.ShapeDtypeStruct(array.shape, array.dtype),
        in_specs=[ANY] * (1 + len(tokens)),
        out_specs=ANY,
        input_output_aliases={0: 0},
        compiler_params=pltpu.CompilerParams(vmem_limit_bytes=VMEM_LIMIT),
    )(array, *tokens)


def rows_kernel(block_ref, *refs, low):
    out_ref, held, in_sem, out_sem = refs[-4:]
    size = held.shape[0]
    ins = [pltpu.make_async_copy(rows_at(block_ref, low + k), held.at[k], in_sem.at[k]) for k in range(size)]
    outs = [pltpu.make_async_copy(held.at[k], rows_at(out_ref, k), out_sem.at[k]) for k in range(size)]
    for copy in ins:
        copy.start()
    for copy, out in zip(ins, outs):
        copy.wait()
        out.start()
    for out in outs:
        out.wait()


def rows_after(block, low, size, *tokens):
    cols = block.shape[1]
    return pl.pallas_call(
        functools.partial(rows_kernel, low=low),
        out_shape=jax.ShapeDtypeStruct((size * ROWBLK, cols), block.dtype),
        in_specs=[HBM] + [ANY] * len(tokens),
        out_specs=ANY,
        scratch_shapes=[
            pltpu.VMEM((size, ROWBLK, cols), block.dtype),
            pltpu.SemaphoreType.DMA((size,)),
            pltpu.SemaphoreType.DMA((size,)),
        ],
        compiler_params=pltpu.CompilerParams(vmem_limit_bytes=VMEM_ALL),
    )(block, *tokens)


def pick_kernel(position_ref, edge_ref, inner_ref, *refs, sizes):
    outs, (held, in_sem, out_sem) = refs[: len(sizes)], refs[len(sizes) :]
    place = lax.rem(position_ref[0], LEVEL)
    inner = (place == 1) | (place == 2)
    copies = []
    for out, at in [(out, at) for out, size in zip(outs, sizes) for at in range(size)]:
        k = len(copies)
        pl.when(inner)(pltpu.make_async_copy(rows_at(inner_ref, k), held.at[k], in_sem.at[k]).start)
        pl.when(jnp.logical_not(inner))(pltpu.make_async_copy(rows_at(edge_ref, k), held.at[k], in_sem.at[k]).start)
        copies.append(pltpu.make_async_copy(held.at[k], rows_at(out, at), out_sem.at[k]))
    for k, copy in enumerate(copies):
        pltpu.make_async_copy(rows_at(edge_ref, k), held.at[k], in_sem.at[k]).wait()
        copy.start()
    for copy in copies:
        copy.wait()


def pick(position, edge, inner, sizes, *tokens):
    rows, cols = edge.shape
    total = rows // ROWBLK

    def body(position_ref, edge_ref, inner_ref, *refs):
        pick_kernel(position_ref, edge_ref, inner_ref, *refs[len(tokens) :], sizes=sizes)

    return pl.pallas_call(
        body,
        out_shape=tuple(jax.ShapeDtypeStruct((size * ROWBLK, cols), edge.dtype) for size in sizes),
        in_specs=[SMEM] + [ANY] * (2 + len(tokens)),
        out_specs=(ANY,) * len(sizes),
        scratch_shapes=[
            pltpu.VMEM((total, ROWBLK, cols), edge.dtype),
            pltpu.SemaphoreType.DMA((total,)),
            pltpu.SemaphoreType.DMA((total,)),
        ],
        compiler_params=pltpu.CompilerParams(vmem_limit_bytes=VMEM_LIMIT),
    )(position, edge, inner, *tokens)


def own_kernel(position_ref, live_ref, sig_ref, own_ref, diag_ref, own_t_ref, own, own_t, tile, in_sem, turned_sem, out_sem, *, block_total):
    steps = own.shape[0]
    geo = Geometry(position_ref, live_ref, sig_ref, block_total)
    count = geo.live(geo.me)

    def in_copy(r):
        return pltpu.make_async_copy(rows_at(own_ref, r), own.at[r], in_sem.at[r])

    def turned_copy(r):
        return pltpu.make_async_copy(own_t.at[r], own_t_ref.at[r], turned_sem.at[r])

    for r in range(steps):
        pl.when(r < count)(in_copy(r).start)
    tile[...] = jnp.zeros_like(tile)

    @pl.loop(0, count)
    def _(r):
        in_copy(r).wait()
        own_t[r] = own[r].T
        turned_copy(r).start()
        dot_into(tile, own_t[r], own[r])

    start_tile(tile, diag_ref.at[0], out_sem.at[0])

    @pl.loop(0, count)
    def _(r):
        turned_copy(r).wait()

    wait_tile(tile, out_sem.at[0])


def own_tile(scalars, own, block_total):
    rows, cols = own.shape
    steps = rows // ROWBLK
    return pl.pallas_call(
        functools.partial(own_kernel, block_total=block_total),
        out_shape=(
            jax.ShapeDtypeStruct((1, cols, cols), jnp.float32),
            jax.ShapeDtypeStruct((steps, cols, ROWBLK), own.dtype),
        ),
        in_specs=[SMEM] * 3 + [ANY],
        out_specs=(ANY,) * 2,
        scratch_shapes=[
            pltpu.VMEM((steps, ROWBLK, cols), own.dtype),
            pltpu.VMEM((steps, cols, ROWBLK), own.dtype),
            pltpu.VMEM((cols, cols), jnp.float32),
            pltpu.SemaphoreType.DMA((steps,)),
            pltpu.SemaphoreType.DMA((steps,)),
            pltpu.SemaphoreType.DMA((1,)),
        ],
        compiler_params=pltpu.CompilerParams(vmem_limit_bytes=VMEM_LIMIT),
        cost_estimate=pl.CostEstimate(
            flops=2 * rows * cols * cols, bytes_accessed=4 * rows * cols + 4 * cols * cols, transcendentals=0
        ),
    )(*scalars, own)


def core_kernel(
    position_ref, live_ref, sig_ref, core_ref, own_t_ref, up_ref, low_ref, core_t_ref, _token, own_t, core, core_t, tile, sems,
    turned_sem, out_sem, *, block_total,
):
    steps = core.shape[0]
    geo = Geometry(position_ref, live_ref, sig_ref, block_total)
    core_count = geo.live(geo.core)
    pair_count = geo.count(geo.me, geo.core)

    def core_copy(r):
        return pltpu.make_async_copy(rows_at(core_ref, r), core.at[r], sems.at[0, r])

    def own_copy(r):
        return pltpu.make_async_copy(own_t_ref.at[r], own_t.at[r], sems.at[1, r])

    def turned_copy(r):
        return pltpu.make_async_copy(core_t.at[r], core_t_ref.at[r], turned_sem.at[r])

    for r in range(steps):
        pl.when(r < core_count)(core_copy(r).start)
        pl.when(r < pair_count)(own_copy(r).start)
    tile[...] = jnp.zeros_like(tile)

    @pl.loop(0, core_count)
    def _(r):
        core_copy(r).wait()
        core_t[r] = core[r].T
        turned_copy(r).start()

        @pl.when(r < pair_count)
        def _():
            own_copy(r).wait()
            dot_into(tile, own_t[r], core[r])

    geo.place_tile(tile, geo.core, up_ref, low_ref, out_sem.at[0])

    @pl.loop(0, core_count)
    def _(r):
        turned_copy(r).wait()

    wait_tile(tile, out_sem.at[0])


def core_tile(scalars, core, own_t, block_total):
    rows, cols = core.shape
    steps = rows // ROWBLK
    three = jax.ShapeDtypeStruct((1, HOPS, cols, cols), jnp.float32)
    return pl.pallas_call(
        functools.partial(core_kernel, block_total=block_total),
        out_shape=(three, three, jax.ShapeDtypeStruct(own_t.shape, own_t.dtype), TOKEN),
        in_specs=[SMEM] * 3 + [ANY] * 2,
        out_specs=(ANY,) * 4,
        scratch_shapes=[
            pltpu.VMEM((steps, cols, ROWBLK), core.dtype),
            pltpu.VMEM((steps, ROWBLK, cols), core.dtype),
            pltpu.VMEM((steps, cols, ROWBLK), core.dtype),
            pltpu.VMEM((cols, cols), jnp.float32),
            pltpu.SemaphoreType.DMA((2, steps)),
            pltpu.SemaphoreType.DMA((steps,)),
            pltpu.SemaphoreType.DMA((1,)),
        ],
        compiler_params=pltpu.CompilerParams(vmem_limit_bytes=VMEM_LIMIT),
        cost_estimate=pl.CostEstimate(
            flops=2 * rows * cols * cols, bytes_accessed=6 * rows * cols + 4 * cols * cols, transcendentals=0
        ),
    )(*scalars, core, own_t)


def pair_kernel(
    position_ref, live_ref, sig_ref, own_t_ref, core_t_ref, piece_refs, before, outs, own_t, core_t, held, tiles, sems,
    before_sem, out_sem, *, which, low, high, sources, final, block_total,
):
    geo = Geometry(position_ref, live_ref, sig_ref, block_total)
    other = getattr(geo, which)
    shared = which != "far"
    count = geo.count(geo.me, other)
    core_count = geo.count(geo.core, other) if shared else 0
    either = jnp.maximum(count, core_count)

    for r in range(low, high):
        at, (ref, offset) = r - low, sources[r]
        own_copy = pltpu.make_async_copy(own_t_ref.at[r], own_t.at[at], sems.at[0, at])
        pl.when(r < count)(own_copy.start)
        if shared:
            core_copy = pltpu.make_async_copy(core_t_ref.at[r], core_t.at[at], sems.at[1, at])
            pl.when(r < core_count)(core_copy.start)
        held_copy = pltpu.make_async_copy(rows_at(piece_refs[ref], offset), held.at[at], sems.at[2, at])
        pl.when(r < either)(held_copy.start)

    if before:
        for i in range(2):
            start_tile(before[i], tiles.at[i], before_sem.at[i])
        for i in range(2):
            wait_tile(tiles.at[i], before_sem.at[i])
    else:
        tiles[...] = jnp.zeros_like(tiles)

    @pl.loop(0, high - low)
    def _(at):
        r = at + low

        @pl.when(r < either)
        def _():
            pltpu.make_async_copy(rows_at(piece_refs[0], 0), held.at[at], sems.at[2, at]).wait()

        @pl.when(r < count)
        def _():
            pltpu.make_async_copy(own_t_ref.at[0], own_t.at[at], sems.at[0, at]).wait()
            dot_into(tiles.at[0], own_t[at], held[at])

        if shared:
            @pl.when(r < core_count)
            def _():
                pltpu.make_async_copy(core_t_ref.at[0], core_t.at[at], sems.at[1, at]).wait()
                dot_into(tiles.at[1], core_t[at], held[at])

    if shared:
        start_tile(tiles.at[1], outs[-1], out_sem.at[1])
    if final:
        geo.place_tile(tiles.at[0], other, outs[0], outs[1], out_sem.at[0])
        wait_tile(tiles.at[0], out_sem.at[0])
    else:
        start_tile(tiles.at[0], outs[0], out_sem.at[0])
        wait_tile(tiles.at[0], out_sem.at[0])
    if shared:
        wait_tile(tiles.at[1], out_sem.at[1])


def pair_tiles(scalars, turned, which, pieces, low, high, before, outputs, block_total):
    steps, cols, _ = turned[0].shape
    tile = jax.ShapeDtypeStruct((cols, cols), jnp.float32)
    final = outputs is not None
    places = [(i, k) for i, piece in enumerate(pieces) for k in range(piece.shape[0] // ROWBLK)]
    sources = dict(zip(range(low, high), places))
    before, chained = list(before or ()), list(outputs or ())
    n_in, n_before = len(pieces), len(before)
    n_out = (2 if final else 1) + (which != "far")

    def body(position_ref, live_ref, sig_ref, own_t_ref, core_t_ref, *refs):
        outs_at = n_in + n_before + len(chained)
        pair_kernel(
            position_ref, live_ref, sig_ref, own_t_ref, core_t_ref, refs[:n_in], refs[n_in : n_in + n_before],
            refs[outs_at : outs_at + n_out], *refs[outs_at + n_out + 1 :],
            which=which, low=low, high=high, sources=sources, final=final, block_total=block_total,
        )

    span = high - low
    return pl.pallas_call(
        body,
        out_shape=tuple(jax.ShapeDtypeStruct(c.shape, c.dtype) for c in chained) + (tile,) * (n_out - len(chained)) + (TOKEN,),
        in_specs=[SMEM] * 3 + [ANY] * (2 + n_in + n_before + len(chained)),
        out_specs=(ANY,) * (n_out + 1),
        scratch_shapes=[pltpu.VMEM((span, cols, ROWBLK), turned[0].dtype)] * 2
        + [
            pltpu.VMEM((span, ROWBLK, cols), turned[0].dtype),
            pltpu.VMEM((2, cols, cols), jnp.float32),
            pltpu.SemaphoreType.DMA((3, span)),
            pltpu.SemaphoreType.DMA((2,)),
            pltpu.SemaphoreType.DMA((2,)),
        ],
        input_output_aliases={5 + n_in + n_before + i: i for i in range(len(chained))},
        compiler_params=pltpu.CompilerParams(vmem_limit_bytes=VMEM_LIMIT),
        cost_estimate=pl.CostEstimate(
            flops=4 * span * ROWBLK * cols * cols,
            bytes_accessed=6 * span * ROWBLK * cols + 16 * cols * cols,
            transcendentals=0,
        ),
    )(*scalars, *turned, *pieces, *before, *chained)


def end_kernel(
    position_ref, live_ref, sig_ref, own_t_ref, pieces, before, up_ref, low_ref, _token, own_t, held, tiles, own_sem, held_sem,
    before_sem, out_sem, *, names, low, block_total,
):
    span = own_t.shape[0]
    geo = Geometry(position_ref, live_ref, sig_ref, block_total)
    others = [getattr(geo, name) for name in names]
    counts = [geo.count(geo.me, other) - low for other in others]
    either = functools.reduce(jnp.maximum, counts)

    def own_copy(at):
        return pltpu.make_async_copy(own_t_ref.at[low + at], own_t.at[at], own_sem.at[at])

    def held_copy(rows, i, at):
        return pltpu.make_async_copy(rows, held.at[i, at], held_sem.at[i, at])

    for i in range(len(names)):
        start_tile(before[i], tiles.at[i], before_sem.at[i])
        for at in range(span):
            if i == 0:
                pl.when(at < either)(own_copy(at).start)
            pl.when(at < counts[i])(held_copy(pieces[i][at], i, at).start)
    for at in range(span):
        pl.when(at < either)(own_copy(at).wait)
    for i in range(len(names)):
        wait_tile(tiles.at[i], before_sem.at[i])

        @pl.loop(0, jnp.maximum(counts[i], 0))
        def _(at):
            held_copy(pieces[i][0], i, at).wait()
            dot_into(tiles.at[i], own_t[at], held[i, at])

        geo.place_tile(tiles.at[i], others[i], up_ref, low_ref, out_sem.at[i])
    for i in range(len(names)):
        wait_tile(tiles.at[i], out_sem.at[i])


def end_tiles(scalars, own_t, jobs, low, outputs, block_total):
    steps, cols, _ = own_t.shape
    span, n = steps - low, len(jobs)
    names = [job[0] for job in jobs]
    pieces = [piece for job in jobs for piece in job[1]]
    before = [job[2] for job in jobs]
    places = [(p, k) for p, piece in enumerate(pieces) for k in range(piece.shape[0] // ROWBLK)]
    n_in = len(pieces)

    def body(position_ref, live_ref, sig_ref, own_t_ref, *refs):
        rows = [rows_at(refs[p], k) for p, k in places]
        end_kernel(
            position_ref, live_ref, sig_ref, own_t_ref, [rows[i * span : (i + 1) * span] for i in range(n)],
            refs[n_in : n_in + n], *refs[n_in + n + 2 :],
            names=names, low=low, block_total=block_total,
        )

    return pl.pallas_call(
        body,
        out_shape=(*(jax.ShapeDtypeStruct(o.shape, o.dtype) for o in outputs), TOKEN),
        in_specs=[SMEM] * 3 + [ANY] * (3 + n_in + n),
        out_specs=(ANY,) * 3,
        scratch_shapes=[
            pltpu.VMEM((span, cols, ROWBLK), own_t.dtype),
            pltpu.VMEM((n, span, ROWBLK, cols), own_t.dtype),
            pltpu.VMEM((n, cols, cols), jnp.float32),
            pltpu.SemaphoreType.DMA((span,)),
            pltpu.SemaphoreType.DMA((n, span)),
            pltpu.SemaphoreType.DMA((n,)),
            pltpu.SemaphoreType.DMA((n,)),
        ],
        input_output_aliases={4 + n_in + n: 0, 5 + n_in + n: 1},
        compiler_params=pltpu.CompilerParams(vmem_limit_bytes=VMEM_LIMIT),
        cost_estimate=pl.CostEstimate(
            flops=2 * n * span * ROWBLK * cols * cols,
            bytes_accessed=2 * (n + 1) * span * ROWBLK * cols + 8 * n * cols * cols,
            transcendentals=0,
        ),
    )(*scalars, own_t, *pieces, *before, *outputs)


def per_device(b_half, significant, live_rows):
    block_total = lax.axis_size("ao")
    position = lax.axis_index("ao").astype(jnp.int32)[None]
    scalars = (position, live_rows, significant)
    steps = b_half.shape[0] // ROWBLK

    def send(block, moves):
        return lax.ppermute(block, "ao", level_route(block_total, moves))

    cores = [(j, 0, j ^ 1) for j in range(LEVEL)]
    across = [(j, 0, j ^ 2) for j in range(LEVEL)]
    far = [(1, 1, 0), (0, -1, 1), (3, 1, 2), (2, -1, 3)]
    relay = [(0, 1, 0), (1, 1, 1), (2, -1, 2), (3, -1, 3)]
    turn = [(0, 1, 0), (3, -1, 3), (1, 0, 2), (2, 0, 1)]

    head = rows_after(b_half, 0, HEAD)
    y_head = send(head, across)
    tail = rows_after(b_half, HEAD, steps - HEAD, head)
    y_tail = send(tail, across)
    far_head, far_tail = send(head, far), send(tail, far)
    core = send(b_half, cores)

    diagonal, own_t = own_tile(scalars, b_half, block_total)
    upper, lower, core_t, made_core = core_tile(scalars, core, own_t, block_total)
    turned = (own_t, core_t)
    y_head = after(y_head, made_core)
    relayed = send(y_head, relay)
    y_part, both_part, made_y = pair_tiles(scalars, turned, "across", [y_head], 0, HEAD, None, None, block_total)
    both_part = send(both_part, cores)
    upper, lower, made_far = pair_tiles(
        scalars, turned, "far", [far_head, far_tail], 0, steps, None, (upper, lower), block_total
    )

    y_tail = after(y_tail, made_y, made_far)
    relay_tail = [send(piece, turn) for piece in pick(position, y_tail, far_tail, TURNS)]
    both_tail = send(y_tail, cores)
    relay_part, last_part, made_relay = pair_tiles(
        scalars, turned, "relay", [relayed], 0, HEAD, None, None, block_total
    )
    last_part = send(last_part, cores)
    jobs = [("across", [y_tail], y_part), ("both", [both_tail], both_part)]
    upper, lower, made_across = end_tiles(scalars, own_t, jobs, HEAD, (upper, lower), block_total)

    relay_tail[0] = after(relay_tail[0], made_across, made_relay)
    last_tail = [send(piece, cores) for piece in relay_tail]
    jobs = [("relay", relay_tail, relay_part), ("last", last_tail, last_part)]
    upper, lower, _ = end_tiles(scalars, own_t, jobs, HEAD, (upper, lower), block_total)
    return diagonal, upper, lower


def solution(mesh):
    in_specs = (P("groups", "ao"), P("groups", None), P("groups"))
    out_specs = (
        P(("groups", "ao"), None, None),
        P(("groups", "ao"), None, None, None),
        P(("groups", "ao"), None, None, None),
    )
    return jax.shard_map(
        per_device, mesh=mesh, in_specs=in_specs, out_specs=out_specs, check_vma=False
    )
```

```python
import functools

import jax
import jax.numpy as jnp
from jax import lax
from jax.experimental import pallas as pl
from jax.experimental.pallas import tpu as pltpu
from jax.sharding import PartitionSpec as P

ROWBLK = 512
HOPS = 3
VMEM_LIMIT = 28 * 2**20
VMEM_ALL = 63 * 2**20
LEVEL = 4
PARTS = 4

SMEM = pl.BlockSpec(memory_space=pltpu.SMEM)
HBM = pl.BlockSpec(memory_space=pltpu.HBM)
ANY = pl.BlockSpec(memory_space=pl.ANY)
VMEM = pl.BlockSpec(memory_space=pltpu.VMEM)
TOKEN = jax.ShapeDtypeStruct((8, 128), jnp.float32)


def level_route(block_total, moves):
    levels = block_total // LEVEL
    return [
        (LEVEL * z + place, LEVEL * (z + step) + new)
        for z in range(levels)
        for place, step, new in moves
        if 0 <= z + step < levels
    ]


def start_tile(source, target, sem):
    rows = source.shape[0] // PARTS
    for part in range(PARTS):
        at = pl.ds(part * rows, rows)
        pltpu.make_async_copy(source.at[at], target.at[at], sem).start()


def wait_tile(tile, sem):
    pltpu.make_async_copy(tile, tile, sem).wait()


class Geometry:
    def __init__(self, position_ref, live_ref, sig_ref, block_total):
        self.live_ref, self.sig_ref, self.block_total = live_ref, sig_ref, block_total
        self.me = position_ref if live_ref is None else position_ref[0]
        self.place = lax.rem(self.me, LEVEL)
        even = lax.rem(self.place, 2) == 0
        self.upper = self.place >= 2
        self.edge = (self.place == 0) | (self.place == 3)
        self.core = self.me + jnp.where(even, 1, -1)
        self.across = self.me + jnp.where(self.upper, -2, 2)
        self.far = self.me + jnp.where(even, -3, 3)
        self.relay = self.me + jnp.where(self.upper, 2, -2)
        self.both = self.me + (LEVEL - 1) - 2 * self.place
        self.last = self.me + jnp.where(self.edge, 1, 3) * jnp.where(self.upper, 1, -1)

    def live(self, block):
        return self.live_ref[jnp.clip(block, 0, self.block_total - 1)] // ROWBLK

    def count(self, first, second):
        low = jnp.clip(jnp.minimum(first, second), 0, self.block_total - 1)
        hop = jnp.clip(jnp.abs(first - second) - 1, 0, HOPS - 1)
        inside = (second >= 0) & (second < self.block_total)
        rows = jnp.minimum(self.live(first), self.live(second))
        return jnp.where(inside, rows * self.sig_ref[low, hop], 0)

    def place_tile(self, tile, other, up_ref, low_ref, sem, enable=True):
        dist = other - self.me
        hop = jnp.clip(jnp.abs(dist) - 1, 0, HOPS - 1)

        @pl.when(enable & (dist > 0))
        def _():
            start_tile(tile, up_ref.at[0, hop], sem)

        @pl.when(enable & (dist < 0))
        def _():
            start_tile(tile, low_ref.at[0, hop], sem)


def rows_at(ref, r):
    return ref.at[pl.ds(r * ROWBLK, ROWBLK)]


def dot_into(total, left, right):
    total[...] += jnp.dot(left, right, preferred_element_type=jnp.float32)


def gate_kernel(*refs):
    del refs


def after(array, *tokens):
    return pl.pallas_call(
        gate_kernel,
        out_shape=jax.ShapeDtypeStruct(array.shape, array.dtype),
        in_specs=[ANY] * (1 + len(tokens)),
        out_specs=ANY,
        input_output_aliases={0: 0},
        compiler_params=pltpu.CompilerParams(vmem_limit_bytes=VMEM_LIMIT),
    )(array, *tokens)


def rows_kernel(block_ref, *refs, low):
    out_ref, held, in_sem, out_sem = refs[-4:]
    size = held.shape[0]
    part = held.shape[1]
    ins, outs = [], []
    for k in range(size):
        source, target = pl.ds(low * ROWBLK + k * part, part), pl.ds(k * part, part)
        ins.append(pltpu.make_async_copy(block_ref.at[source], held.at[k], in_sem.at[k]))
        outs.append(pltpu.make_async_copy(held.at[k], out_ref.at[target], out_sem.at[k]))
    for copy in ins:
        copy.start()
    for copy, out in zip(ins, outs):
        copy.wait()
        out.start()
    for out in outs:
        out.wait()


def rows_after(block, low, size, *tokens):
    cols = block.shape[1]
    return pl.pallas_call(
        functools.partial(rows_kernel, low=low),
        out_shape=jax.ShapeDtypeStruct((size * ROWBLK, cols), block.dtype),
        in_specs=[HBM] + [ANY] * len(tokens),
        out_specs=ANY,
        scratch_shapes=[
            pltpu.VMEM((4 * size, ROWBLK // 4, cols), block.dtype),
            pltpu.SemaphoreType.DMA((4 * size,)),
            pltpu.SemaphoreType.DMA((4 * size,)),
        ],
        compiler_params=pltpu.CompilerParams(vmem_limit_bytes=VMEM_ALL),
    )(block, *tokens)


def pick_kernel(position_ref, edge_ref, inner_ref, *refs, sizes):
    outs, (held, in_sem, out_sem) = refs[: len(sizes)], refs[len(sizes) :]
    place = lax.rem(position_ref[0], LEVEL)
    inner = (place == 1) | (place == 2)
    copies = []
    for out, at in [(out, at) for out, size in zip(outs, sizes) for at in range(size)]:
        k = len(copies)
        pl.when(inner)(pltpu.make_async_copy(rows_at(inner_ref, k), held.at[k], in_sem.at[k]).start)
        pl.when(jnp.logical_not(inner))(pltpu.make_async_copy(rows_at(edge_ref, k), held.at[k], in_sem.at[k]).start)
        copies.append(pltpu.make_async_copy(held.at[k], rows_at(out, at), out_sem.at[k]))
    for k, copy in enumerate(copies):
        pltpu.make_async_copy(rows_at(edge_ref, k), held.at[k], in_sem.at[k]).wait()
        copy.start()
    for copy in copies:
        copy.wait()


def pick(position, edge, inner, sizes):
    cols = edge.shape[1]
    total = sum(sizes)
    return pl.pallas_call(
        functools.partial(pick_kernel, sizes=sizes),
        out_shape=tuple(jax.ShapeDtypeStruct((size * ROWBLK, cols), edge.dtype) for size in sizes),
        in_specs=[SMEM] + [ANY] * 2,
        out_specs=(ANY,) * len(sizes),
        scratch_shapes=[
            pltpu.VMEM((total, ROWBLK, cols), edge.dtype),
            pltpu.SemaphoreType.DMA((total,)),
            pltpu.SemaphoreType.DMA((total,)),
        ],
        compiler_params=pltpu.CompilerParams(vmem_limit_bytes=VMEM_LIMIT),
    )(position, edge, inner)


def own_kernel(position_ref, live_ref, sig_ref, own_ref, diag_ref, own_t_ref, own, own_t, tile, in_sem, turned_sem, out_sem, *, block_total):
    steps = own.shape[0]
    geo = Geometry(position_ref, live_ref, sig_ref, block_total)
    count = geo.live(geo.me)

    def in_copy(r):
        return pltpu.make_async_copy(rows_at(own_ref, r), own.at[r], in_sem.at[r])

    def turned_copy(r):
        return pltpu.make_async_copy(own_t.at[r], own_t_ref.at[r], turned_sem.at[r])

    for r in range(steps):
        pl.when(r < count)(in_copy(r).start)
    tile[...] = jnp.zeros_like(tile)

    @pl.loop(0, count)
    def _(r):
        in_copy(r).wait()
        own_t[r] = own[r].T
        turned_copy(r).start()
        dot_into(tile, own_t[r], own[r])

    start_tile(tile, diag_ref.at[0], out_sem.at[0])

    @pl.loop(0, count)
    def _(r):
        turned_copy(r).wait()

    wait_tile(tile, out_sem.at[0])


def own_tile(scalars, own, block_total):
    rows, cols = own.shape
    steps = rows // ROWBLK
    return pl.pallas_call(
        functools.partial(own_kernel, block_total=block_total),
        out_shape=(
            jax.ShapeDtypeStruct((1, cols, cols), jnp.float32),
            jax.ShapeDtypeStruct((steps, cols, ROWBLK), own.dtype),
        ),
        in_specs=[SMEM] * 3 + [ANY],
        out_specs=(ANY,) * 2,
        scratch_shapes=[
            pltpu.VMEM((steps, ROWBLK, cols), own.dtype),
            pltpu.VMEM((steps, cols, ROWBLK), own.dtype),
            pltpu.VMEM((cols, cols), jnp.float32),
            pltpu.SemaphoreType.DMA((steps,)),
            pltpu.SemaphoreType.DMA((steps,)),
            pltpu.SemaphoreType.DMA((1,)),
        ],
        compiler_params=pltpu.CompilerParams(vmem_limit_bytes=VMEM_LIMIT),
        cost_estimate=pl.CostEstimate(
            flops=2 * rows * cols * cols, bytes_accessed=4 * rows * cols + 4 * cols * cols, transcendentals=0
        ),
    )(*scalars, own)


def core_kernel(
    position_ref, live_ref, sig_ref, core_ref, own_t_ref, up_ref, low_ref, core_t_ref, _token, own_t, core, core_t, tile, sems,
    turned_sem, out_sem, *, block_total,
):
    steps = core.shape[0]
    geo = Geometry(position_ref, live_ref, sig_ref, block_total)
    core_count = geo.live(geo.core)
    pair_count = geo.count(geo.me, geo.core)

    def core_copy(r):
        return pltpu.make_async_copy(rows_at(core_ref, r), core.at[r], sems.at[0, r])

    def own_copy(r):
        return pltpu.make_async_copy(own_t_ref.at[r], own_t.at[r], sems.at[1, r])

    def turned_copy(r):
        return pltpu.make_async_copy(core_t.at[r], core_t_ref.at[r], turned_sem.at[r])

    for r in range(steps):
        pl.when(r < core_count)(core_copy(r).start)
        pl.when(r < pair_count)(own_copy(r).start)
    tile[...] = jnp.zeros_like(tile)

    @pl.loop(0, core_count)
    def _(r):
        core_copy(r).wait()
        core_t[r] = core[r].T
        turned_copy(r).start()

        @pl.when(r < pair_count)
        def _():
            own_copy(r).wait()
            dot_into(tile, own_t[r], core[r])

    geo.place_tile(tile, geo.core, up_ref, low_ref, out_sem.at[0])

    @pl.loop(0, core_count)
    def _(r):
        turned_copy(r).wait()

    wait_tile(tile, out_sem.at[0])


def core_tile(scalars, core, own_t, block_total):
    rows, cols = core.shape
    steps = rows // ROWBLK
    three = jax.ShapeDtypeStruct((1, HOPS, cols, cols), jnp.float32)
    return pl.pallas_call(
        functools.partial(core_kernel, block_total=block_total),
        out_shape=(three, three, jax.ShapeDtypeStruct(own_t.shape, own_t.dtype), TOKEN),
        in_specs=[SMEM] * 3 + [ANY] * 2,
        out_specs=(ANY,) * 4,
        scratch_shapes=[
            pltpu.VMEM((steps, cols, ROWBLK), core.dtype),
            pltpu.VMEM((steps, ROWBLK, cols), core.dtype),
            pltpu.VMEM((steps, cols, ROWBLK), core.dtype),
            pltpu.VMEM((cols, cols), jnp.float32),
            pltpu.SemaphoreType.DMA((2, steps)),
            pltpu.SemaphoreType.DMA((steps,)),
            pltpu.SemaphoreType.DMA((1,)),
        ],
        compiler_params=pltpu.CompilerParams(vmem_limit_bytes=VMEM_LIMIT),
        cost_estimate=pl.CostEstimate(
            flops=2 * rows * cols * cols, bytes_accessed=6 * rows * cols + 4 * cols * cols, transcendentals=0
        ),
    )(*scalars, core, own_t)


def pair_kernel(
    position_ref, live_ref, sig_ref, own_t_ref, core_t_ref, piece_refs, before, outs, own_t, core_t, held, tiles, sems,
    before_sem, out_sem, *, which, low, high, sources, final, block_total,
):
    geo = Geometry(position_ref, live_ref, sig_ref, block_total)
    other = getattr(geo, which)
    shared = which != "far"
    count = geo.count(geo.me, other)
    core_count = geo.count(geo.core, other) if shared else 0
    either = jnp.maximum(count, core_count)

    for r in range(low, high):
        at, (ref, offset) = r - low, sources[r]
        own_copy = pltpu.make_async_copy(own_t_ref.at[r], own_t.at[at], sems.at[0, at])
        pl.when(r < count)(own_copy.start)
        if shared:
            core_copy = pltpu.make_async_copy(core_t_ref.at[r], core_t.at[at], sems.at[1, at])
            pl.when(r < core_count)(core_copy.start)
        held_copy = pltpu.make_async_copy(rows_at(piece_refs[ref], offset), held.at[at], sems.at[2, at])
        pl.when(r < either)(held_copy.start)

    if before:
        for i in range(2):
            start_tile(before[i], tiles.at[i], before_sem.at[i])
        for i in range(2):
            wait_tile(tiles.at[i], before_sem.at[i])
    else:
        tiles[...] = jnp.zeros_like(tiles)

    @pl.loop(0, high - low)
    def _(at):
        r = at + low

        @pl.when(r < either)
        def _():
            pltpu.make_async_copy(rows_at(piece_refs[0], 0), held.at[at], sems.at[2, at]).wait()

        @pl.when(r < count)
        def _():
            pltpu.make_async_copy(own_t_ref.at[0], own_t.at[at], sems.at[0, at]).wait()
            dot_into(tiles.at[0], own_t[at], held[at])

        if shared:
            @pl.when(r < core_count)
            def _():
                pltpu.make_async_copy(core_t_ref.at[0], core_t.at[at], sems.at[1, at]).wait()
                dot_into(tiles.at[1], core_t[at], held[at])

    if shared:
        start_tile(tiles.at[1], outs[-1], out_sem.at[1])
    if final:
        geo.place_tile(tiles.at[0], other, outs[0], outs[1], out_sem.at[0])
        wait_tile(tiles.at[0], out_sem.at[0])
    else:
        start_tile(tiles.at[0], outs[0], out_sem.at[0])
        wait_tile(tiles.at[0], out_sem.at[0])
    if shared:
        wait_tile(tiles.at[1], out_sem.at[1])


def pair_tiles(scalars, turned, which, pieces, low, high, before, outputs, block_total):
    steps, cols, _ = turned[0].shape
    tile = jax.ShapeDtypeStruct((cols, cols), jnp.float32)
    final = outputs is not None
    places = [(i, k) for i, piece in enumerate(pieces) for k in range(piece.shape[0] // ROWBLK)]
    sources = dict(zip(range(low, high), places))
    before, chained = list(before or ()), list(outputs or ())
    n_in, n_before = len(pieces), len(before)
    n_out = (2 if final else 1) + (which != "far")

    def body(position_ref, live_ref, sig_ref, own_t_ref, core_t_ref, *refs):
        outs_at = n_in + n_before + len(chained)
        pair_kernel(
            position_ref, live_ref, sig_ref, own_t_ref, core_t_ref, refs[:n_in], refs[n_in : n_in + n_before],
            refs[outs_at : outs_at + n_out], *refs[outs_at + n_out + 1 :],
            which=which, low=low, high=high, sources=sources, final=final, block_total=block_total,
        )

    span = high - low
    return pl.pallas_call(
        body,
        out_shape=tuple(jax.ShapeDtypeStruct(c.shape, c.dtype) for c in chained) + (tile,) * (n_out - len(chained)) + (TOKEN,),
        in_specs=[SMEM] * 3 + [ANY] * (2 + n_in + n_before + len(chained)),
        out_specs=(ANY,) * (n_out + 1),
        scratch_shapes=[pltpu.VMEM((span, cols, ROWBLK), turned[0].dtype)] * 2
        + [
            pltpu.VMEM((span, ROWBLK, cols), turned[0].dtype),
            pltpu.VMEM((2, cols, cols), jnp.float32),
            pltpu.SemaphoreType.DMA((3, span)),
            pltpu.SemaphoreType.DMA((2,)),
            pltpu.SemaphoreType.DMA((2,)),
        ],
        input_output_aliases={5 + n_in + n_before + i: i for i in range(len(chained))},
        compiler_params=pltpu.CompilerParams(vmem_limit_bytes=VMEM_LIMIT),
        cost_estimate=pl.CostEstimate(
            flops=4 * span * ROWBLK * cols * cols,
            bytes_accessed=6 * span * ROWBLK * cols + 16 * cols * cols,
            transcendentals=0,
        ),
    )(*scalars, *turned, *pieces, *before, *chained)


def end_kernel(
    position_ref, live_ref, sig_ref, own_t_ref, pieces, before, up_ref, low_ref, _token, tiles, out_sem, *, names, low,
    block_total,
):
    geo = Geometry(position_ref, live_ref, sig_ref, block_total)
    for i, name in enumerate(names):
        other = getattr(geo, name)
        count = geo.count(geo.me, other) - low
        tiles[i] = before[i][...]
        for at, rows in enumerate(pieces[i]):
            @pl.when(at < count)
            def _():
                dot_into(tiles.at[i], own_t_ref[low + at], rows[...])

        geo.place_tile(tiles.at[i], other, up_ref, low_ref, out_sem.at[i])
    for i in range(len(names)):
        wait_tile(tiles.at[i], out_sem.at[i])


def add_kernel(
    position_ref, live_ref, sig_ref, own_t_ref, pieces, before, outs, *, names, low, left, block_total,
):
    geo = Geometry(position_ref, live_ref, sig_ref, block_total)
    tiles, masked = outs[: len(names)], outs[len(names) :]
    for i, name in enumerate(names):
        count = geo.count(geo.me, getattr(geo, name)) - low
        tiles[i][...] = before[i][...]
        for at, rows in enumerate(pieces[i]):
            @pl.when(at < count)
            def _():
                dot_into(tiles[i], own_t_ref[low + at], rows[...])

        for k in range(left):
            at = len(pieces[i]) + k
            kept = own_t_ref[low + at]
            masked[i][k] = jnp.where(at < count, kept, jnp.zeros_like(kept))


def last_kernel(masked, pieces, before, up_ref, low_ref, tiles, out_sem, *, names, block_total):
    geo = Geometry(lax.axis_index("ao"), None, None, block_total)
    for i, name in enumerate(names):
        total = before[i][...]
        for k, rows in enumerate(pieces[i]):
            total += jnp.dot(masked[i][k], rows[...], preferred_element_type=jnp.float32)
        tiles[i] = total
        geo.place_tile(tiles.at[i], getattr(geo, name), up_ref, low_ref, out_sem.at[i])
    for i in range(len(names)):
        wait_tile(tiles.at[i], out_sem.at[i])


def split_jobs(jobs):
    pieces = [piece for job in jobs for piece in job[1]]
    places = [(p, k) for p, piece in enumerate(pieces) for k in range(piece.shape[0] // ROWBLK)]
    span = len(places) // len(jobs)

    def rows_of(refs):
        rows = [rows_at(refs[p], k) for p, k in places]
        return [rows[i * span : (i + 1) * span] for i in range(len(jobs))]

    return [job[0] for job in jobs], pieces, [job[2] for job in jobs], span, rows_of


def end_cost(n, span, cols):
    return pl.CostEstimate(
        flops=2 * n * span * ROWBLK * cols * cols,
        bytes_accessed=2 * (n + 1) * span * ROWBLK * cols + 8 * n * cols * cols,
        transcendentals=0,
    )


def end_tiles(scalars, own_t, jobs, low, outputs, block_total):
    cols, n = own_t.shape[1], len(jobs)
    names, pieces, before, span, rows_of = split_jobs(jobs)
    n_in = len(pieces)

    def body(position_ref, live_ref, sig_ref, own_t_ref, *refs):
        end_kernel(
            position_ref, live_ref, sig_ref, own_t_ref, rows_of(refs), refs[n_in : n_in + n], *refs[n_in + n + 2 :],
            names=names, low=low, block_total=block_total,
        )

    return pl.pallas_call(
        body,
        out_shape=(*(jax.ShapeDtypeStruct(o.shape, o.dtype) for o in outputs), TOKEN),
        in_specs=[SMEM] * 3 + [VMEM] * (1 + n_in + n) + [ANY] * 2,
        out_specs=(ANY,) * 3,
        scratch_shapes=[pltpu.VMEM((n, cols, cols), jnp.float32), pltpu.SemaphoreType.DMA((n,))],
        input_output_aliases={4 + n_in + n: 0, 5 + n_in + n: 1},
        compiler_params=pltpu.CompilerParams(vmem_limit_bytes=VMEM_LIMIT),
        cost_estimate=end_cost(n, span, cols),
    )(*scalars, own_t, *pieces, *before, *outputs)


def add_rows(scalars, own_t, jobs, low, left, block_total):
    cols, n = own_t.shape[1], len(jobs)
    names, pieces, before, span, rows_of = split_jobs(jobs)
    n_in = len(pieces)

    def body(position_ref, live_ref, sig_ref, own_t_ref, *refs):
        add_kernel(
            position_ref, live_ref, sig_ref, own_t_ref, rows_of(refs), refs[n_in : n_in + n], refs[n_in + n :],
            names=names, low=low, left=left, block_total=block_total,
        )

    masked = jax.ShapeDtypeStruct((left, *own_t.shape[1:]), own_t.dtype)
    outs = pl.pallas_call(
        body,
        out_shape=tuple(jax.ShapeDtypeStruct(tile.shape, tile.dtype) for tile in before) + (masked,) * n,
        in_specs=[SMEM] * 3 + [VMEM] * (1 + n_in + n),
        out_specs=(VMEM,) * (2 * n),
        compiler_params=pltpu.CompilerParams(vmem_limit_bytes=VMEM_LIMIT),
        cost_estimate=end_cost(n, span, cols),
    )(*scalars, own_t, *pieces, *before)
    return outs[:n], outs[n:]


def last_tiles(masked, jobs, outputs, block_total):
    cols, n = masked[0].shape[1], len(jobs)
    names, pieces, before, span, rows_of = split_jobs(jobs)
    n_in = len(pieces)

    def body(*refs):
        last_kernel(
            refs[:n], rows_of(refs[n:]), refs[n + n_in : 2 * n + n_in], *refs[2 * n + n_in + 2 :],
            names=names, block_total=block_total,
        )

    return pl.pallas_call(
        body,
        out_shape=tuple(jax.ShapeDtypeStruct(o.shape, o.dtype) for o in outputs),
        in_specs=[VMEM] * (2 * n + n_in) + [ANY] * 2,
        out_specs=(ANY,) * 2,
        scratch_shapes=[pltpu.VMEM((n, cols, cols), jnp.float32), pltpu.SemaphoreType.DMA((n,))],
        input_output_aliases={2 * n + n_in: 0, 2 * n + n_in + 1: 1},
        compiler_params=pltpu.CompilerParams(vmem_limit_bytes=VMEM_LIMIT),
        cost_estimate=end_cost(n, span, cols),
    )(*masked, *pieces, *before, *outputs)


def plan(total, head, turns, block_total, b_half, position, live_rows, significant):
    scalars = (position, live_rows, significant)

    def send(block, moves):
        return lax.ppermute(block, "ao", level_route(block_total, moves))

    cores = [(j, 0, j ^ 1) for j in range(LEVEL)]
    across = [(j, 0, j ^ 2) for j in range(LEVEL)]
    far = [(1, 1, 0), (0, -1, 1), (3, 1, 2), (2, -1, 3)]
    relay = [(0, 1, 0), (1, 1, 1), (2, -1, 2), (3, -1, 3)]
    turn = [(0, 1, 0), (3, -1, 3), (1, 0, 2), (2, 0, 1)]

    first = rows_after(b_half, 0, head)
    y_head = send(first, across)
    later = rows_after(b_half, head, total - head, first)
    y_tail = send(later, across)
    far_head, far_tail = send(first, far), send(later, far)
    core = send(b_half, cores)

    diagonal, own_t = own_tile(scalars, b_half, block_total)
    upper, lower, core_t, made_core = core_tile(scalars, core, own_t, block_total)
    turned = (own_t, core_t)
    y_head = after(y_head, made_core)
    relayed = send(y_head, relay)
    y_part, both_part, made_y = pair_tiles(scalars, turned, "across", [y_head], 0, head, None, None, block_total)
    both_part = send(both_part, cores)
    upper, lower, made_far = pair_tiles(
        scalars, turned, "far", [far_head, far_tail], 0, total, None, (upper, lower), block_total
    )

    y_tail = after(y_tail, made_y, made_far)
    relay_tail = [send(piece, turn) for piece in pick(position, y_tail, far_tail, turns)]
    both_tail = send(y_tail, cores)
    relay_part, last_part, made_relay = pair_tiles(
        scalars, turned, "relay", [relayed], 0, head, None, None, block_total
    )
    last_part = send(last_part, cores)
    jobs = [("across", [y_tail], y_part), ("both", [both_tail], both_part)]
    upper, lower, made_across = end_tiles(scalars, own_t, jobs, head, (upper, lower), block_total)

    relay_tail[:2] = [after(piece, made_across, made_relay) for piece in relay_tail[:2]]
    last_tail = [send(piece, cores) for piece in relay_tail]
    jobs = [("relay", relay_tail[:-1], relay_part), ("last", last_tail[:-1], last_part)]
    (relay_part, last_part), masked = add_rows(scalars, own_t, jobs, head, turns[-1], block_total)
    jobs = [("relay", relay_tail[-1:], relay_part), ("last", last_tail[-1:], last_part)]
    upper, lower = last_tiles(masked, jobs, (upper, lower), block_total)
    return diagonal, upper, lower


def per_device(b_half, significant, live_rows):
    block_total = lax.axis_size("ao")
    position = lax.axis_index("ao").astype(jnp.int32)[None]
    steps = b_half.shape[0] // ROWBLK
    return plan(steps, 3, (1, 1, 1), block_total, b_half, position, live_rows, significant)


def solution(mesh):
    in_specs = (P("groups", "ao"), P("groups", None), P("groups"))
    out_specs = (
        P(("groups", "ao"), None, None),
        P(("groups", "ao"), None, None, None),
        P(("groups", "ao"), None, None, None),
    )
    return jax.shard_map(
        per_device, mesh=mesh, in_specs=in_specs, out_specs=out_specs, check_vma=False
    )
```

```python
import functools

import jax
import jax.numpy as jnp
from jax import lax
from jax.experimental import pallas as pl
from jax.experimental.pallas import tpu as pltpu
from jax.sharding import PartitionSpec as P

ROWBLK = 512
HOPS = 3
VMEM_LIMIT = 28 * 2**20
VMEM_ALL = 63 * 2**20
LEVEL = 4
PARTS = 4

SMEM = pl.BlockSpec(memory_space=pltpu.SMEM)
HBM = pl.BlockSpec(memory_space=pltpu.HBM)
ANY = pl.BlockSpec(memory_space=pl.ANY)
VMEM = pl.BlockSpec(memory_space=pltpu.VMEM)
TOKEN = jax.ShapeDtypeStruct((8, 128), jnp.float32)


def level_route(block_total, moves):
    levels = block_total // LEVEL
    return [
        (LEVEL * z + place, LEVEL * (z + step) + new)
        for z in range(levels)
        for place, step, new in moves
        if 0 <= z + step < levels
    ]


def start_tile(source, target, sem):
    rows = source.shape[0] // PARTS
    for part in range(PARTS):
        at = pl.ds(part * rows, rows)
        pltpu.make_async_copy(source.at[at], target.at[at], sem).start()


def wait_tile(tile, sem):
    pltpu.make_async_copy(tile, tile, sem).wait()


class Geometry:
    def __init__(self, position_ref, live_ref, sig_ref, block_total):
        self.live_ref, self.sig_ref, self.block_total = live_ref, sig_ref, block_total
        self.me = position_ref if live_ref is None else position_ref[0]
        self.place = lax.rem(self.me, LEVEL)
        even = lax.rem(self.place, 2) == 0
        self.upper = self.place >= 2
        self.edge = (self.place == 0) | (self.place == 3)
        self.core = self.me + jnp.where(even, 1, -1)
        self.across = self.me + jnp.where(self.upper, -2, 2)
        self.far = self.me + jnp.where(even, -3, 3)
        self.relay = self.me + jnp.where(self.upper, 2, -2)
        self.both = self.me + (LEVEL - 1) - 2 * self.place
        self.last = self.me + jnp.where(self.edge, 1, 3) * jnp.where(self.upper, 1, -1)

    def live(self, block):
        return self.live_ref[jnp.clip(block, 0, self.block_total - 1)] // ROWBLK

    def count(self, first, second):
        low = jnp.clip(jnp.minimum(first, second), 0, self.block_total - 1)
        hop = jnp.clip(jnp.abs(first - second) - 1, 0, HOPS - 1)
        inside = (second >= 0) & (second < self.block_total)
        rows = jnp.minimum(self.live(first), self.live(second))
        return jnp.where(inside, rows * self.sig_ref[low, hop], 0)

    def place_tile(self, tile, other, up_ref, low_ref, sem, enable=True):
        dist = other - self.me
        hop = jnp.clip(jnp.abs(dist) - 1, 0, HOPS - 1)

        @pl.when(enable & (dist > 0))
        def _():
            start_tile(tile, up_ref.at[0, hop], sem)

        @pl.when(enable & (dist < 0))
        def _():
            start_tile(tile, low_ref.at[0, hop], sem)


def rows_at(ref, r):
    return ref.at[pl.ds(r * ROWBLK, ROWBLK)]


def dot_into(total, left, right):
    total[...] += jnp.dot(left, right, preferred_element_type=jnp.float32)


def gate_kernel(*refs):
    del refs


def after(array, *tokens):
    return pl.pallas_call(
        gate_kernel,
        out_shape=jax.ShapeDtypeStruct(array.shape, array.dtype),
        in_specs=[ANY] * (1 + len(tokens)),
        out_specs=ANY,
        input_output_aliases={0: 0},
        compiler_params=pltpu.CompilerParams(vmem_limit_bytes=VMEM_LIMIT),
    )(array, *tokens)


def rows_kernel(block_ref, *refs, low):
    out_ref, held, in_sem, out_sem = refs[-4:]
    size = held.shape[0]
    part = held.shape[1]
    ins, outs = [], []
    for k in range(size):
        source, target = pl.ds(low * ROWBLK + k * part, part), pl.ds(k * part, part)
        ins.append(pltpu.make_async_copy(block_ref.at[source], held.at[k], in_sem.at[k]))
        outs.append(pltpu.make_async_copy(held.at[k], out_ref.at[target], out_sem.at[k]))
    for copy in ins:
        copy.start()
    for copy, out in zip(ins, outs):
        copy.wait()
        out.start()
    for out in outs:
        out.wait()


def rows_after(block, low, size, *tokens):
    cols = block.shape[1]
    return pl.pallas_call(
        functools.partial(rows_kernel, low=low),
        out_shape=jax.ShapeDtypeStruct((size * ROWBLK, cols), block.dtype),
        in_specs=[HBM] + [ANY] * len(tokens),
        out_specs=ANY,
        scratch_shapes=[
            pltpu.VMEM((4 * size, ROWBLK // 4, cols), block.dtype),
            pltpu.SemaphoreType.DMA((4 * size,)),
            pltpu.SemaphoreType.DMA((4 * size,)),
        ],
        compiler_params=pltpu.CompilerParams(vmem_limit_bytes=VMEM_ALL),
    )(block, *tokens)


def pick_kernel(position_ref, edge_ref, inner_ref, *refs, sizes):
    outs, (held, in_sem, out_sem) = refs[: len(sizes)], refs[len(sizes) :]
    place = lax.rem(position_ref[0], LEVEL)
    inner = (place == 1) | (place == 2)
    copies = []
    for out, at in [(out, at) for out, size in zip(outs, sizes) for at in range(size)]:
        k = len(copies)
        pl.when(inner)(pltpu.make_async_copy(rows_at(inner_ref, k), held.at[k], in_sem.at[k]).start)
        pl.when(jnp.logical_not(inner))(pltpu.make_async_copy(rows_at(edge_ref, k), held.at[k], in_sem.at[k]).start)
        copies.append(pltpu.make_async_copy(held.at[k], rows_at(out, at), out_sem.at[k]))
    for k, copy in enumerate(copies):
        pltpu.make_async_copy(rows_at(edge_ref, k), held.at[k], in_sem.at[k]).wait()
        copy.start()
    for copy in copies:
        copy.wait()


def pick(position, edge, inner, sizes):
    cols = edge.shape[1]
    total = sum(sizes)
    return pl.pallas_call(
        functools.partial(pick_kernel, sizes=sizes),
        out_shape=tuple(jax.ShapeDtypeStruct((size * ROWBLK, cols), edge.dtype) for size in sizes),
        in_specs=[SMEM] + [ANY] * 2,
        out_specs=(ANY,) * len(sizes),
        scratch_shapes=[
            pltpu.VMEM((total, ROWBLK, cols), edge.dtype),
            pltpu.SemaphoreType.DMA((total,)),
            pltpu.SemaphoreType.DMA((total,)),
        ],
        compiler_params=pltpu.CompilerParams(vmem_limit_bytes=VMEM_LIMIT),
    )(position, edge, inner)


def own_kernel(position_ref, live_ref, sig_ref, own_ref, diag_ref, own_t_ref, own, own_t, tile, in_sem, turned_sem, out_sem, *, block_total):
    steps = own.shape[0]
    geo = Geometry(position_ref, live_ref, sig_ref, block_total)
    count = geo.live(geo.me)

    def in_copy(r):
        return pltpu.make_async_copy(rows_at(own_ref, r), own.at[r], in_sem.at[r])

    def turned_copy(r):
        return pltpu.make_async_copy(own_t.at[r], own_t_ref.at[r], turned_sem.at[r])

    for r in range(steps):
        pl.when(r < count)(in_copy(r).start)
    tile[...] = jnp.zeros_like(tile)

    @pl.loop(0, count)
    def _(r):
        in_copy(r).wait()
        own_t[r] = own[r].T
        turned_copy(r).start()
        dot_into(tile, own_t[r], own[r])

    start_tile(tile, diag_ref.at[0], out_sem.at[0])

    @pl.loop(0, count)
    def _(r):
        turned_copy(r).wait()

    wait_tile(tile, out_sem.at[0])


def own_tile(scalars, own, block_total):
    rows, cols = own.shape
    steps = rows // ROWBLK
    return pl.pallas_call(
        functools.partial(own_kernel, block_total=block_total),
        out_shape=(
            jax.ShapeDtypeStruct((1, cols, cols), jnp.float32),
            jax.ShapeDtypeStruct((steps, cols, ROWBLK), own.dtype),
        ),
        in_specs=[SMEM] * 3 + [ANY],
        out_specs=(ANY,) * 2,
        scratch_shapes=[
            pltpu.VMEM((steps, ROWBLK, cols), own.dtype),
            pltpu.VMEM((steps, cols, ROWBLK), own.dtype),
            pltpu.VMEM((cols, cols), jnp.float32),
            pltpu.SemaphoreType.DMA((steps,)),
            pltpu.SemaphoreType.DMA((steps,)),
            pltpu.SemaphoreType.DMA((1,)),
        ],
        compiler_params=pltpu.CompilerParams(vmem_limit_bytes=VMEM_LIMIT),
        cost_estimate=pl.CostEstimate(
            flops=2 * rows * cols * cols, bytes_accessed=4 * rows * cols + 4 * cols * cols, transcendentals=0
        ),
    )(*scalars, own)


def core_kernel(
    position_ref, live_ref, sig_ref, core_ref, own_t_ref, up_ref, low_ref, core_t_ref, _token, own_t, core, core_t, tile, sems,
    turned_sem, out_sem, *, block_total,
):
    steps = core.shape[0]
    geo = Geometry(position_ref, live_ref, sig_ref, block_total)
    core_count = geo.live(geo.core)
    pair_count = geo.count(geo.me, geo.core)

    def core_copy(r):
        return pltpu.make_async_copy(rows_at(core_ref, r), core.at[r], sems.at[0, r])

    def own_copy(r):
        return pltpu.make_async_copy(own_t_ref.at[r], own_t.at[r], sems.at[1, r])

    def turned_copy(r):
        return pltpu.make_async_copy(core_t.at[r], core_t_ref.at[r], turned_sem.at[r])

    for r in range(steps):
        pl.when(r < core_count)(core_copy(r).start)
        pl.when(r < pair_count)(own_copy(r).start)
    tile[...] = jnp.zeros_like(tile)

    @pl.loop(0, core_count)
    def _(r):
        core_copy(r).wait()
        core_t[r] = core[r].T
        turned_copy(r).start()

        @pl.when(r < pair_count)
        def _():
            own_copy(r).wait()
            dot_into(tile, own_t[r], core[r])

    geo.place_tile(tile, geo.core, up_ref, low_ref, out_sem.at[0])

    @pl.loop(0, core_count)
    def _(r):
        turned_copy(r).wait()

    wait_tile(tile, out_sem.at[0])


def core_tile(scalars, core, own_t, block_total):
    rows, cols = core.shape
    steps = rows // ROWBLK
    three = jax.ShapeDtypeStruct((1, HOPS, cols, cols), jnp.float32)
    return pl.pallas_call(
        functools.partial(core_kernel, block_total=block_total),
        out_shape=(three, three, jax.ShapeDtypeStruct(own_t.shape, own_t.dtype), TOKEN),
        in_specs=[SMEM] * 3 + [ANY] * 2,
        out_specs=(ANY,) * 4,
        scratch_shapes=[
            pltpu.VMEM((steps, cols, ROWBLK), core.dtype),
            pltpu.VMEM((steps, ROWBLK, cols), core.dtype),
            pltpu.VMEM((steps, cols, ROWBLK), core.dtype),
            pltpu.VMEM((cols, cols), jnp.float32),
            pltpu.SemaphoreType.DMA((2, steps)),
            pltpu.SemaphoreType.DMA((steps,)),
            pltpu.SemaphoreType.DMA((1,)),
        ],
        compiler_params=pltpu.CompilerParams(vmem_limit_bytes=VMEM_LIMIT),
        cost_estimate=pl.CostEstimate(
            flops=2 * rows * cols * cols, bytes_accessed=6 * rows * cols + 4 * cols * cols, transcendentals=0
        ),
    )(*scalars, core, own_t)


def pair_kernel(
    position_ref, live_ref, sig_ref, own_t_ref, core_t_ref, piece_refs, before, outs, own_t, core_t, held, tiles, sems,
    before_sem, out_sem, *, which, low, high, sources, final, block_total,
):
    geo = Geometry(position_ref, live_ref, sig_ref, block_total)
    other = getattr(geo, which)
    shared = which != "far"
    count = geo.count(geo.me, other)
    core_count = geo.count(geo.core, other) if shared else 0
    either = jnp.maximum(count, core_count)

    for r in range(low, high):
        at, (ref, offset) = r - low, sources[r]
        own_copy = pltpu.make_async_copy(own_t_ref.at[r], own_t.at[at], sems.at[0, at])
        pl.when(r < count)(own_copy.start)
        if shared:
            core_copy = pltpu.make_async_copy(core_t_ref.at[r], core_t.at[at], sems.at[1, at])
            pl.when(r < core_count)(core_copy.start)
        held_copy = pltpu.make_async_copy(rows_at(piece_refs[ref], offset), held.at[at], sems.at[2, at])
        pl.when(r < either)(held_copy.start)

    if before:
        for i in range(2):
            start_tile(before[i], tiles.at[i], before_sem.at[i])
        for i in range(2):
            wait_tile(tiles.at[i], before_sem.at[i])
    else:
        tiles[...] = jnp.zeros_like(tiles)

    @pl.loop(0, high - low)
    def _(at):
        r = at + low

        @pl.when(r < either)
        def _():
            pltpu.make_async_copy(rows_at(piece_refs[0], 0), held.at[at], sems.at[2, at]).wait()

        @pl.when(r < count)
        def _():
            pltpu.make_async_copy(own_t_ref.at[0], own_t.at[at], sems.at[0, at]).wait()
            dot_into(tiles.at[0], own_t[at], held[at])

        if shared:
            @pl.when(r < core_count)
            def _():
                pltpu.make_async_copy(core_t_ref.at[0], core_t.at[at], sems.at[1, at]).wait()
                dot_into(tiles.at[1], core_t[at], held[at])

    if shared:
        start_tile(tiles.at[1], outs[-1], out_sem.at[1])
    if final:
        geo.place_tile(tiles.at[0], other, outs[0], outs[1], out_sem.at[0])
        wait_tile(tiles.at[0], out_sem.at[0])
    else:
        start_tile(tiles.at[0], outs[0], out_sem.at[0])
        wait_tile(tiles.at[0], out_sem.at[0])
    if shared:
        wait_tile(tiles.at[1], out_sem.at[1])


def pair_tiles(scalars, turned, which, pieces, low, high, before, outputs, block_total):
    steps, cols, _ = turned[0].shape
    tile = jax.ShapeDtypeStruct((cols, cols), jnp.float32)
    final = outputs is not None
    places = [(i, k) for i, piece in enumerate(pieces) for k in range(piece.shape[0] // ROWBLK)]
    sources = dict(zip(range(low, high), places))
    before, chained = list(before or ()), list(outputs or ())
    n_in, n_before = len(pieces), len(before)
    n_out = (2 if final else 1) + (which != "far")

    def body(position_ref, live_ref, sig_ref, own_t_ref, core_t_ref, *refs):
        outs_at = n_in + n_before + len(chained)
        pair_kernel(
            position_ref, live_ref, sig_ref, own_t_ref, core_t_ref, refs[:n_in], refs[n_in : n_in + n_before],
            refs[outs_at : outs_at + n_out], *refs[outs_at + n_out + 1 :],
            which=which, low=low, high=high, sources=sources, final=final, block_total=block_total,
        )

    span = high - low
    return pl.pallas_call(
        body,
        out_shape=tuple(jax.ShapeDtypeStruct(c.shape, c.dtype) for c in chained) + (tile,) * (n_out - len(chained)) + (TOKEN,),
        in_specs=[SMEM] * 3 + [ANY] * (2 + n_in + n_before + len(chained)),
        out_specs=(ANY,) * (n_out + 1),
        scratch_shapes=[pltpu.VMEM((span, cols, ROWBLK), turned[0].dtype)] * 2
        + [
            pltpu.VMEM((span, ROWBLK, cols), turned[0].dtype),
            pltpu.VMEM((2, cols, cols), jnp.float32),
            pltpu.SemaphoreType.DMA((3, span)),
            pltpu.SemaphoreType.DMA((2,)),
            pltpu.SemaphoreType.DMA((2,)),
        ],
        input_output_aliases={5 + n_in + n_before + i: i for i in range(len(chained))},
        compiler_params=pltpu.CompilerParams(vmem_limit_bytes=VMEM_LIMIT),
        cost_estimate=pl.CostEstimate(
            flops=4 * span * ROWBLK * cols * cols,
            bytes_accessed=6 * span * ROWBLK * cols + 16 * cols * cols,
            transcendentals=0,
        ),
    )(*scalars, *turned, *pieces, *before, *chained)


def end_kernel(
    position_ref, live_ref, sig_ref, own_t_ref, pieces, before, up_ref, low_ref, _token, tiles, out_sem, *, names, low,
    block_total,
):
    geo = Geometry(position_ref, live_ref, sig_ref, block_total)
    for i, name in enumerate(names):
        other = getattr(geo, name)
        count = geo.count(geo.me, other) - low
        tiles[i] = before[i][...]
        for at, rows in enumerate(pieces[i]):
            @pl.when(at < count)
            def _():
                dot_into(tiles.at[i], own_t_ref[low + at], rows[...])

        geo.place_tile(tiles.at[i], other, up_ref, low_ref, out_sem.at[i])
    for i in range(len(names)):
        wait_tile(tiles.at[i], out_sem.at[i])


def mask_kernel(position_ref, live_ref, sig_ref, own_t_ref, *masked, names, low, block_total):
    geo = Geometry(position_ref, live_ref, sig_ref, block_total)
    for out_ref, name in zip(masked, names):
        count = geo.count(geo.me, getattr(geo, name)) - low
        for k in range(out_ref.shape[0]):
            kept = own_t_ref[low + k]
            out_ref[k] = jnp.where(k < count, kept, jnp.zeros_like(kept))


def mask_rows(scalars, own_t, names, low, block_total):
    masked = jax.ShapeDtypeStruct((own_t.shape[0] - low, *own_t.shape[1:]), own_t.dtype)
    return pl.pallas_call(
        functools.partial(mask_kernel, names=names, low=low, block_total=block_total),
        out_shape=(masked,) * len(names),
        in_specs=[SMEM] * 3 + [VMEM],
        out_specs=(VMEM,) * len(names),
        compiler_params=pltpu.CompilerParams(vmem_limit_bytes=VMEM_LIMIT),
    )(*scalars, own_t)


def add_kernel(masked, pieces, before, outs):
    for i, out_ref in enumerate(outs):
        total = before[i][...]
        for k, rows in enumerate(pieces[i]):
            total += jnp.dot(masked[i][k], rows[...], preferred_element_type=jnp.float32)
        out_ref[...] = total


def last_kernel(masked, pieces, before, up_ref, low_ref, tiles, out_sem, *, names, first, block_total):
    geo = Geometry(lax.axis_index("ao"), None, None, block_total)
    for i, name in enumerate(names):
        total = before[i][...]
        for k, rows in enumerate(pieces[i]):
            total += jnp.dot(masked[i][first + k], rows[...], preferred_element_type=jnp.float32)
        tiles[i] = total
        geo.place_tile(tiles.at[i], getattr(geo, name), up_ref, low_ref, out_sem.at[i])
    for i in range(len(names)):
        wait_tile(tiles.at[i], out_sem.at[i])


def split_jobs(jobs):
    pieces = [piece for job in jobs for piece in job[1]]
    places = [(p, k) for p, piece in enumerate(pieces) for k in range(piece.shape[0] // ROWBLK)]
    span = len(places) // len(jobs)

    def rows_of(refs):
        rows = [rows_at(refs[p], k) for p, k in places]
        return [rows[i * span : (i + 1) * span] for i in range(len(jobs))]

    return [job[0] for job in jobs], pieces, [job[2] for job in jobs], span, rows_of


def end_cost(n, span, cols):
    return pl.CostEstimate(
        flops=2 * n * span * ROWBLK * cols * cols,
        bytes_accessed=2 * (n + 1) * span * ROWBLK * cols + 8 * n * cols * cols,
        transcendentals=0,
    )


def end_tiles(scalars, own_t, jobs, low, outputs, block_total):
    cols, n = own_t.shape[1], len(jobs)
    names, pieces, before, span, rows_of = split_jobs(jobs)
    n_in = len(pieces)

    def body(position_ref, live_ref, sig_ref, own_t_ref, *refs):
        end_kernel(
            position_ref, live_ref, sig_ref, own_t_ref, rows_of(refs), refs[n_in : n_in + n], *refs[n_in + n + 2 :],
            names=names, low=low, block_total=block_total,
        )

    return pl.pallas_call(
        body,
        out_shape=(*(jax.ShapeDtypeStruct(o.shape, o.dtype) for o in outputs), TOKEN),
        in_specs=[SMEM] * 3 + [VMEM] * (1 + n_in + n) + [ANY] * 2,
        out_specs=(ANY,) * 3,
        scratch_shapes=[pltpu.VMEM((n, cols, cols), jnp.float32), pltpu.SemaphoreType.DMA((n,))],
        input_output_aliases={4 + n_in + n: 0, 5 + n_in + n: 1},
        compiler_params=pltpu.CompilerParams(vmem_limit_bytes=VMEM_LIMIT),
        cost_estimate=end_cost(n, span, cols),
    )(*scalars, own_t, *pieces, *before, *outputs)


def add_rows(masked, jobs):
    cols, n = masked[0].shape[1], len(jobs)
    _, pieces, before, span, rows_of = split_jobs(jobs)
    n_in = len(pieces)

    def body(*refs):
        add_kernel(refs[:n], rows_of(refs[n:]), refs[n + n_in : 2 * n + n_in], refs[2 * n + n_in :])

    return pl.pallas_call(
        body,
        out_shape=tuple(jax.ShapeDtypeStruct(tile.shape, tile.dtype) for tile in before),
        in_specs=[VMEM] * (2 * n + n_in),
        out_specs=(VMEM,) * n,
        compiler_params=pltpu.CompilerParams(vmem_limit_bytes=VMEM_LIMIT),
        cost_estimate=end_cost(n, span, cols),
    )(*masked, *pieces, *before)


def last_tiles(masked, jobs, first, outputs, block_total):
    cols, n = masked[0].shape[1], len(jobs)
    names, pieces, before, span, rows_of = split_jobs(jobs)
    n_in = len(pieces)

    def body(*refs):
        last_kernel(
            refs[:n], rows_of(refs[n:]), refs[n + n_in : 2 * n + n_in], *refs[2 * n + n_in + 2 :],
            names=names, first=first, block_total=block_total,
        )

    return pl.pallas_call(
        body,
        out_shape=tuple(jax.ShapeDtypeStruct(o.shape, o.dtype) for o in outputs),
        in_specs=[VMEM] * (2 * n + n_in) + [ANY] * 2,
        out_specs=(ANY,) * 2,
        scratch_shapes=[pltpu.VMEM((n, cols, cols), jnp.float32), pltpu.SemaphoreType.DMA((n,))],
        input_output_aliases={2 * n + n_in: 0, 2 * n + n_in + 1: 1},
        compiler_params=pltpu.CompilerParams(vmem_limit_bytes=VMEM_LIMIT),
        cost_estimate=end_cost(n, span, cols),
    )(*masked, *pieces, *before, *outputs)


def plan(total, head, turns, block_total, b_half, position, live_rows, significant):
    scalars = (position, live_rows, significant)

    def send(block, moves):
        return lax.ppermute(block, "ao", level_route(block_total, moves))

    cores = [(j, 0, j ^ 1) for j in range(LEVEL)]
    across = [(j, 0, j ^ 2) for j in range(LEVEL)]
    far = [(1, 1, 0), (0, -1, 1), (3, 1, 2), (2, -1, 3)]
    relay = [(0, 1, 0), (1, 1, 1), (2, -1, 2), (3, -1, 3)]
    turn = [(0, 1, 0), (3, -1, 3), (1, 0, 2), (2, 0, 1)]

    first = rows_after(b_half, 0, head)
    y_head = send(first, across)
    later = rows_after(b_half, head, total - head, first)
    y_tail = send(later, across)
    far_head, far_tail = send(first, far), send(later, far)
    core = send(b_half, cores)

    diagonal, own_t = own_tile(scalars, b_half, block_total)
    upper, lower, core_t, made_core = core_tile(scalars, core, own_t, block_total)
    turned = (own_t, core_t)
    y_head = after(y_head, made_core)
    relayed = send(y_head, relay)
    y_part, both_part, made_y = pair_tiles(scalars, turned, "across", [y_head], 0, head, None, None, block_total)
    both_part = send(both_part, cores)
    upper, lower, made_far = pair_tiles(
        scalars, turned, "far", [far_head, far_tail], 0, total, None, (upper, lower), block_total
    )

    masked = mask_rows(scalars, own_t, ("relay", "last"), head, block_total)
    y_tail = after(y_tail, made_y, made_far, masked[0])
    relay_tail = [send(piece, turn) for piece in pick(position, y_tail, far_tail, turns)]
    both_tail = send(y_tail, cores)
    relay_part, last_part, made_relay = pair_tiles(
        scalars, turned, "relay", [relayed], 0, head, None, None, block_total
    )
    last_part = send(last_part, cores)
    jobs = [("across", [y_tail], y_part), ("both", [both_tail], both_part)]
    upper, lower, made_across = end_tiles(scalars, own_t, jobs, head, (upper, lower), block_total)

    relay_tail[:2] = [after(piece, made_across, made_relay) for piece in relay_tail[:2]]
    last_tail = [send(piece, cores) for piece in relay_tail]
    jobs = [("relay", relay_tail[:-1], relay_part), ("last", last_tail[:-1], last_part)]
    relay_part, last_part = add_rows(masked, jobs)
    jobs = [("relay", relay_tail[-1:], relay_part), ("last", last_tail[-1:], last_part)]
    upper, lower = last_tiles(masked, jobs, sum(turns[:-1]), (upper, lower), block_total)
    return diagonal, upper, lower


def per_device(b_half, significant, live_rows):
    block_total = lax.axis_size("ao")
    position = lax.axis_index("ao").astype(jnp.int32)[None]
    steps = b_half.shape[0] // ROWBLK
    return plan(steps, 3, (1, 1, 1), block_total, b_half, position, live_rows, significant)


def solution(mesh):
    in_specs = (P("groups", "ao"), P("groups", None), P("groups"))
    out_specs = (
        P(("groups", "ao"), None, None),
        P(("groups", "ao"), None, None, None),
        P(("groups", "ao"), None, None, None),
    )
    return jax.shard_map(
        per_device, mesh=mesh, in_specs=in_specs, out_specs=out_specs, check_vma=False
    )
```

```python
import functools

import jax
import jax.numpy as jnp
from jax import lax
from jax.experimental import pallas as pl
from jax.experimental.pallas import tpu as pltpu
from jax.sharding import PartitionSpec as P

ROWBLK = 512
HOPS = 3
VMEM_LIMIT = 28 * 2**20
VMEM_ALL = 63 * 2**20
LEVEL = 4
PARTS = 4

SMEM = pl.BlockSpec(memory_space=pltpu.SMEM)
HBM = pl.BlockSpec(memory_space=pltpu.HBM)
ANY = pl.BlockSpec(memory_space=pl.ANY)
VMEM = pl.BlockSpec(memory_space=pltpu.VMEM)
TOKEN = jax.ShapeDtypeStruct((8, 128), jnp.float32)


def level_route(block_total, moves):
    levels = block_total // LEVEL
    return [
        (LEVEL * z + place, LEVEL * (z + step) + new)
        for z in range(levels)
        for place, step, new in moves
        if 0 <= z + step < levels
    ]


def start_tile(source, target, sem):
    rows = source.shape[0] // PARTS
    for part in range(PARTS):
        at = pl.ds(part * rows, rows)
        pltpu.make_async_copy(source.at[at], target.at[at], sem).start()


def wait_tile(tile, sem):
    pltpu.make_async_copy(tile, tile, sem).wait()


class Geometry:
    def __init__(self, position_ref, live_ref, sig_ref, block_total):
        self.live_ref, self.sig_ref, self.block_total = live_ref, sig_ref, block_total
        self.me = position_ref if live_ref is None else position_ref[0]
        self.place = lax.rem(self.me, LEVEL)
        even = lax.rem(self.place, 2) == 0
        self.upper = self.place >= 2
        self.edge = (self.place == 0) | (self.place == 3)
        self.core = self.me + jnp.where(even, 1, -1)
        self.across = self.me + jnp.where(self.upper, -2, 2)
        self.far = self.me + jnp.where(even, -3, 3)
        self.relay = self.me + jnp.where(self.upper, 2, -2)
        self.both = self.me + (LEVEL - 1) - 2 * self.place
        self.last = self.me + jnp.where(self.edge, 1, 3) * jnp.where(self.upper, 1, -1)

    def live(self, block):
        return self.live_ref[jnp.clip(block, 0, self.block_total - 1)] // ROWBLK

    def count(self, first, second):
        low = jnp.clip(jnp.minimum(first, second), 0, self.block_total - 1)
        hop = jnp.clip(jnp.abs(first - second) - 1, 0, HOPS - 1)
        inside = (second >= 0) & (second < self.block_total)
        rows = jnp.minimum(self.live(first), self.live(second))
        return jnp.where(inside, rows * self.sig_ref[low, hop], 0)

    def place_tile(self, tile, other, up_ref, low_ref, sem, enable=True):
        dist = other - self.me
        hop = jnp.clip(jnp.abs(dist) - 1, 0, HOPS - 1)

        @pl.when(enable & (dist > 0))
        def _():
            start_tile(tile, up_ref.at[0, hop], sem)

        @pl.when(enable & (dist < 0))
        def _():
            start_tile(tile, low_ref.at[0, hop], sem)


def rows_at(ref, r):
    return ref.at[pl.ds(r * ROWBLK, ROWBLK)]


def dot_into(total, left, right):
    total[...] += jnp.dot(left, right, preferred_element_type=jnp.float32)


def gate_kernel(*refs):
    del refs


def after(array, *tokens):
    return pl.pallas_call(
        gate_kernel,
        out_shape=jax.ShapeDtypeStruct(array.shape, array.dtype),
        in_specs=[ANY] * (1 + len(tokens)),
        out_specs=ANY,
        input_output_aliases={0: 0},
        compiler_params=pltpu.CompilerParams(vmem_limit_bytes=VMEM_LIMIT),
    )(array, *tokens)


def rows_kernel(block_ref, *refs, low):
    out_ref, held, in_sem, out_sem = refs[-4:]
    size = held.shape[0]
    part = held.shape[1]
    ins, outs = [], []
    for k in range(size):
        source, target = pl.ds(low * ROWBLK + k * part, part), pl.ds(k * part, part)
        ins.append(pltpu.make_async_copy(block_ref.at[source], held.at[k], in_sem.at[k]))
        outs.append(pltpu.make_async_copy(held.at[k], out_ref.at[target], out_sem.at[k]))
    for copy in ins:
        copy.start()
    for copy, out in zip(ins, outs):
        copy.wait()
        out.start()
    for out in outs:
        out.wait()


def rows_after(block, low, size, *tokens):
    cols = block.shape[1]
    return pl.pallas_call(
        functools.partial(rows_kernel, low=low),
        out_shape=jax.ShapeDtypeStruct((size * ROWBLK, cols), block.dtype),
        in_specs=[HBM] + [ANY] * len(tokens),
        out_specs=ANY,
        scratch_shapes=[
            pltpu.VMEM((4 * size, ROWBLK // 4, cols), block.dtype),
            pltpu.SemaphoreType.DMA((4 * size,)),
            pltpu.SemaphoreType.DMA((4 * size,)),
        ],
        compiler_params=pltpu.CompilerParams(vmem_limit_bytes=VMEM_ALL),
    )(block, *tokens)


def pick_kernel(position_ref, edge_ref, inner_ref, *refs, sizes):
    outs, (held, in_sem, out_sem) = refs[: len(sizes)], refs[len(sizes) :]
    place = lax.rem(position_ref[0], LEVEL)
    inner = (place == 1) | (place == 2)
    copies = []
    for out, at in [(out, at) for out, size in zip(outs, sizes) for at in range(size)]:
        k = len(copies)
        pl.when(inner)(pltpu.make_async_copy(rows_at(inner_ref, k), held.at[k], in_sem.at[k]).start)
        pl.when(jnp.logical_not(inner))(pltpu.make_async_copy(rows_at(edge_ref, k), held.at[k], in_sem.at[k]).start)
        copies.append(pltpu.make_async_copy(held.at[k], rows_at(out, at), out_sem.at[k]))
    for k, copy in enumerate(copies):
        pltpu.make_async_copy(rows_at(edge_ref, k), held.at[k], in_sem.at[k]).wait()
        copy.start()
    for copy in copies:
        copy.wait()


def pick(position, edge, inner, sizes):
    cols = edge.shape[1]
    total = sum(sizes)
    return pl.pallas_call(
        functools.partial(pick_kernel, sizes=sizes),
        out_shape=tuple(jax.ShapeDtypeStruct((size * ROWBLK, cols), edge.dtype) for size in sizes),
        in_specs=[SMEM] + [ANY] * 2,
        out_specs=(ANY,) * len(sizes),
        scratch_shapes=[
            pltpu.VMEM((total, ROWBLK, cols), edge.dtype),
            pltpu.SemaphoreType.DMA((total,)),
            pltpu.SemaphoreType.DMA((total,)),
        ],
        compiler_params=pltpu.CompilerParams(vmem_limit_bytes=VMEM_LIMIT),
    )(position, edge, inner)


def own_kernel(position_ref, live_ref, sig_ref, own_ref, diag_ref, own_t_ref, own, own_t, tile, in_sem, turned_sem, out_sem, *, block_total):
    steps = own.shape[0]
    geo = Geometry(position_ref, live_ref, sig_ref, block_total)
    count = geo.live(geo.me)

    def in_copy(r):
        return pltpu.make_async_copy(rows_at(own_ref, r), own.at[r], in_sem.at[r])

    def turned_copy(r):
        return pltpu.make_async_copy(own_t.at[r], own_t_ref.at[r], turned_sem.at[r])

    for r in range(steps):
        pl.when(r < count)(in_copy(r).start)
    tile[...] = jnp.zeros_like(tile)

    @pl.loop(0, count)
    def _(r):
        in_copy(r).wait()
        own_t[r] = own[r].T
        turned_copy(r).start()
        dot_into(tile, own_t[r], own[r])

    start_tile(tile, diag_ref.at[0], out_sem.at[0])

    @pl.loop(0, count)
    def _(r):
        turned_copy(r).wait()

    wait_tile(tile, out_sem.at[0])


def own_tile(scalars, own, block_total):
    rows, cols = own.shape
    steps = rows // ROWBLK
    return pl.pallas_call(
        functools.partial(own_kernel, block_total=block_total),
        out_shape=(
            jax.ShapeDtypeStruct((1, cols, cols), jnp.float32),
            jax.ShapeDtypeStruct((steps, cols, ROWBLK), own.dtype),
        ),
        in_specs=[SMEM] * 3 + [ANY],
        out_specs=(ANY,) * 2,
        scratch_shapes=[
            pltpu.VMEM((steps, ROWBLK, cols), own.dtype),
            pltpu.VMEM((steps, cols, ROWBLK), own.dtype),
            pltpu.VMEM((cols, cols), jnp.float32),
            pltpu.SemaphoreType.DMA((steps,)),
            pltpu.SemaphoreType.DMA((steps,)),
            pltpu.SemaphoreType.DMA((1,)),
        ],
        compiler_params=pltpu.CompilerParams(vmem_limit_bytes=VMEM_LIMIT),
        cost_estimate=pl.CostEstimate(
            flops=2 * rows * cols * cols, bytes_accessed=4 * rows * cols + 4 * cols * cols, transcendentals=0
        ),
    )(*scalars, own)


def core_kernel(
    position_ref, live_ref, sig_ref, core_ref, own_t_ref, up_ref, low_ref, core_t_ref, _token, own_t, core, core_t, tile, sems,
    turned_sem, out_sem, *, block_total,
):
    steps = core.shape[0]
    geo = Geometry(position_ref, live_ref, sig_ref, block_total)
    core_count = geo.live(geo.core)
    pair_count = geo.count(geo.me, geo.core)

    def core_copy(r):
        return pltpu.make_async_copy(rows_at(core_ref, r), core.at[r], sems.at[0, r])

    def own_copy(r):
        return pltpu.make_async_copy(own_t_ref.at[r], own_t.at[r], sems.at[1, r])

    def turned_copy(r):
        return pltpu.make_async_copy(core_t.at[r], core_t_ref.at[r], turned_sem.at[r])

    for r in range(steps):
        pl.when(r < core_count)(core_copy(r).start)
        pl.when(r < pair_count)(own_copy(r).start)
    tile[...] = jnp.zeros_like(tile)

    @pl.loop(0, core_count)
    def _(r):
        core_copy(r).wait()
        core_t[r] = core[r].T
        turned_copy(r).start()

        @pl.when(r < pair_count)
        def _():
            own_copy(r).wait()
            dot_into(tile, own_t[r], core[r])

    geo.place_tile(tile, geo.core, up_ref, low_ref, out_sem.at[0])

    @pl.loop(0, core_count)
    def _(r):
        turned_copy(r).wait()

    wait_tile(tile, out_sem.at[0])


def core_tile(scalars, core, own_t, block_total):
    rows, cols = core.shape
    steps = rows // ROWBLK
    three = jax.ShapeDtypeStruct((1, HOPS, cols, cols), jnp.float32)
    return pl.pallas_call(
        functools.partial(core_kernel, block_total=block_total),
        out_shape=(three, three, jax.ShapeDtypeStruct(own_t.shape, own_t.dtype), TOKEN),
        in_specs=[SMEM] * 3 + [ANY] * 2,
        out_specs=(ANY,) * 4,
        scratch_shapes=[
            pltpu.VMEM((steps, cols, ROWBLK), core.dtype),
            pltpu.VMEM((steps, ROWBLK, cols), core.dtype),
            pltpu.VMEM((steps, cols, ROWBLK), core.dtype),
            pltpu.VMEM((cols, cols), jnp.float32),
            pltpu.SemaphoreType.DMA((2, steps)),
            pltpu.SemaphoreType.DMA((steps,)),
            pltpu.SemaphoreType.DMA((1,)),
        ],
        compiler_params=pltpu.CompilerParams(vmem_limit_bytes=VMEM_LIMIT),
        cost_estimate=pl.CostEstimate(
            flops=2 * rows * cols * cols, bytes_accessed=6 * rows * cols + 4 * cols * cols, transcendentals=0
        ),
    )(*scalars, core, own_t)


def pair_kernel(
    position_ref, live_ref, sig_ref, own_t_ref, core_t_ref, piece_refs, before, outs, own_t, core_t, held, tiles, sems,
    before_sem, out_sem, *, which, low, high, sources, final, block_total,
):
    geo = Geometry(position_ref, live_ref, sig_ref, block_total)
    other = getattr(geo, which)
    shared = which != "far"
    count = geo.count(geo.me, other)
    core_count = geo.count(geo.core, other) if shared else 0
    either = jnp.maximum(count, core_count)

    for r in range(low, high):
        at, (ref, offset) = r - low, sources[r]
        own_copy = pltpu.make_async_copy(own_t_ref.at[r], own_t.at[at], sems.at[0, at])
        pl.when(r < count)(own_copy.start)
        if shared:
            core_copy = pltpu.make_async_copy(core_t_ref.at[r], core_t.at[at], sems.at[1, at])
            pl.when(r < core_count)(core_copy.start)
        held_copy = pltpu.make_async_copy(rows_at(piece_refs[ref], offset), held.at[at], sems.at[2, at])
        pl.when(r < either)(held_copy.start)

    if before:
        for i in range(2):
            start_tile(before[i], tiles.at[i], before_sem.at[i])
        for i in range(2):
            wait_tile(tiles.at[i], before_sem.at[i])
    else:
        tiles[...] = jnp.zeros_like(tiles)

    @pl.loop(0, high - low)
    def _(at):
        r = at + low

        @pl.when(r < either)
        def _():
            pltpu.make_async_copy(rows_at(piece_refs[0], 0), held.at[at], sems.at[2, at]).wait()

        @pl.when(r < count)
        def _():
            pltpu.make_async_copy(own_t_ref.at[0], own_t.at[at], sems.at[0, at]).wait()
            dot_into(tiles.at[0], own_t[at], held[at])

        if shared:
            @pl.when(r < core_count)
            def _():
                pltpu.make_async_copy(core_t_ref.at[0], core_t.at[at], sems.at[1, at]).wait()
                dot_into(tiles.at[1], core_t[at], held[at])

    if shared:
        start_tile(tiles.at[1], outs[-1], out_sem.at[1])
    if final:
        geo.place_tile(tiles.at[0], other, outs[0], outs[1], out_sem.at[0])
        wait_tile(tiles.at[0], out_sem.at[0])
    else:
        start_tile(tiles.at[0], outs[0], out_sem.at[0])
        wait_tile(tiles.at[0], out_sem.at[0])
    if shared:
        wait_tile(tiles.at[1], out_sem.at[1])


def pair_tiles(scalars, turned, which, pieces, low, high, before, outputs, block_total):
    steps, cols, _ = turned[0].shape
    tile = jax.ShapeDtypeStruct((cols, cols), jnp.float32)
    final = outputs is not None
    places = [(i, k) for i, piece in enumerate(pieces) for k in range(piece.shape[0] // ROWBLK)]
    sources = dict(zip(range(low, high), places))
    before, chained = list(before or ()), list(outputs or ())
    n_in, n_before = len(pieces), len(before)
    n_out = (2 if final else 1) + (which != "far")

    def body(position_ref, live_ref, sig_ref, own_t_ref, core_t_ref, *refs):
        outs_at = n_in + n_before + len(chained)
        pair_kernel(
            position_ref, live_ref, sig_ref, own_t_ref, core_t_ref, refs[:n_in], refs[n_in : n_in + n_before],
            refs[outs_at : outs_at + n_out], *refs[outs_at + n_out + 1 :],
            which=which, low=low, high=high, sources=sources, final=final, block_total=block_total,
        )

    span = high - low
    return pl.pallas_call(
        body,
        out_shape=tuple(jax.ShapeDtypeStruct(c.shape, c.dtype) for c in chained) + (tile,) * (n_out - len(chained)) + (TOKEN,),
        in_specs=[SMEM] * 3 + [ANY] * (2 + n_in + n_before + len(chained)),
        out_specs=(ANY,) * (n_out + 1),
        scratch_shapes=[pltpu.VMEM((span, cols, ROWBLK), turned[0].dtype)] * 2
        + [
            pltpu.VMEM((span, ROWBLK, cols), turned[0].dtype),
            pltpu.VMEM((2, cols, cols), jnp.float32),
            pltpu.SemaphoreType.DMA((3, span)),
            pltpu.SemaphoreType.DMA((2,)),
            pltpu.SemaphoreType.DMA((2,)),
        ],
        input_output_aliases={5 + n_in + n_before + i: i for i in range(len(chained))},
        compiler_params=pltpu.CompilerParams(vmem_limit_bytes=VMEM_LIMIT),
        cost_estimate=pl.CostEstimate(
            flops=4 * span * ROWBLK * cols * cols,
            bytes_accessed=6 * span * ROWBLK * cols + 16 * cols * cols,
            transcendentals=0,
        ),
    )(*scalars, *turned, *pieces, *before, *chained)


def end_kernel(
    position_ref, live_ref, sig_ref, own_t_ref, pieces, before, up_ref, low_ref, _token, tiles, out_sem, *, names, low,
    block_total,
):
    geo = Geometry(position_ref, live_ref, sig_ref, block_total)
    for i, name in enumerate(names):
        other = getattr(geo, name)
        count = geo.count(geo.me, other) - low
        tiles[i] = before[i][...]
        for at, rows in enumerate(pieces[i]):
            @pl.when(at < count)
            def _():
                dot_into(tiles.at[i], own_t_ref[low + at], rows[...])

        geo.place_tile(tiles.at[i], other, up_ref, low_ref, out_sem.at[i])
    for i in range(len(names)):
        wait_tile(tiles.at[i], out_sem.at[i])


def mask_kernel(position_ref, live_ref, sig_ref, own_t_ref, *masked, names, low, block_total):
    geo = Geometry(position_ref, live_ref, sig_ref, block_total)
    for out_ref, name in zip(masked, names):
        count = geo.count(geo.me, getattr(geo, name)) - low
        for k in range(out_ref.shape[0]):
            kept = own_t_ref[low + k]
            out_ref[k] = jnp.where(k < count, kept, jnp.zeros_like(kept))


def mask_rows(scalars, own_t, names, low, block_total):
    masked = jax.ShapeDtypeStruct((own_t.shape[0] - low, *own_t.shape[1:]), own_t.dtype)
    return pl.pallas_call(
        functools.partial(mask_kernel, names=names, low=low, block_total=block_total),
        out_shape=(masked,) * len(names),
        in_specs=[SMEM] * 3 + [VMEM],
        out_specs=(VMEM,) * len(names),
        compiler_params=pltpu.CompilerParams(vmem_limit_bytes=VMEM_LIMIT),
    )(*scalars, own_t)


def add_kernel(masked, pieces, before, outs):
    for i, out_ref in enumerate(outs):
        total = before[i][...]
        for k, rows in enumerate(pieces[i]):
            total += jnp.dot(masked[i][k], rows[...], preferred_element_type=jnp.float32)
        out_ref[...] = total


def last_kernel(masked, pieces, before, up_ref, low_ref, tiles, out_sem, *, names, first, block_total):
    geo = Geometry(lax.axis_index("ao"), None, None, block_total)
    for i, name in enumerate(names):
        total = before[i][...]
        for k, rows in enumerate(pieces[i]):
            total += jnp.dot(masked[i][first + k], rows[...], preferred_element_type=jnp.float32)
        tiles[i] = total
        geo.place_tile(tiles.at[i], getattr(geo, name), up_ref, low_ref, out_sem.at[i])
    for i in range(len(names)):
        wait_tile(tiles.at[i], out_sem.at[i])


def split_jobs(jobs):
    pieces = [piece for job in jobs for piece in job[1]]
    places = [(p, k) for p, piece in enumerate(pieces) for k in range(piece.shape[0] // ROWBLK)]
    span = len(places) // len(jobs)

    def rows_of(refs):
        rows = [rows_at(refs[p], k) for p, k in places]
        return [rows[i * span : (i + 1) * span] for i in range(len(jobs))]

    return [job[0] for job in jobs], pieces, [job[2] for job in jobs], span, rows_of


def end_cost(n, span, cols):
    return pl.CostEstimate(
        flops=2 * n * span * ROWBLK * cols * cols,
        bytes_accessed=2 * (n + 1) * span * ROWBLK * cols + 8 * n * cols * cols,
        transcendentals=0,
    )


def end_tiles(scalars, own_t, jobs, low, outputs, block_total):
    cols, n = own_t.shape[1], len(jobs)
    names, pieces, before, span, rows_of = split_jobs(jobs)
    n_in = len(pieces)

    def body(position_ref, live_ref, sig_ref, own_t_ref, *refs):
        end_kernel(
            position_ref, live_ref, sig_ref, own_t_ref, rows_of(refs), refs[n_in : n_in + n], *refs[n_in + n + 2 :],
            names=names, low=low, block_total=block_total,
        )

    return pl.pallas_call(
        body,
        out_shape=(*(jax.ShapeDtypeStruct(o.shape, o.dtype) for o in outputs), TOKEN),
        in_specs=[SMEM] * 3 + [VMEM] * (1 + n_in + n) + [ANY] * 2,
        out_specs=(ANY,) * 3,
        scratch_shapes=[pltpu.VMEM((n, cols, cols), jnp.float32), pltpu.SemaphoreType.DMA((n,))],
        input_output_aliases={4 + n_in + n: 0, 5 + n_in + n: 1},
        compiler_params=pltpu.CompilerParams(vmem_limit_bytes=VMEM_LIMIT),
        cost_estimate=end_cost(n, span, cols),
    )(*scalars, own_t, *pieces, *before, *outputs)


def add_rows(masked, jobs):
    cols, n = masked[0].shape[1], len(jobs)
    _, pieces, before, span, rows_of = split_jobs(jobs)
    n_in = len(pieces)

    def body(*refs):
        add_kernel(refs[:n], rows_of(refs[n:]), refs[n + n_in : 2 * n + n_in], refs[2 * n + n_in :])

    return pl.pallas_call(
        body,
        out_shape=tuple(jax.ShapeDtypeStruct(tile.shape, tile.dtype) for tile in before),
        in_specs=[VMEM] * (2 * n + n_in),
        out_specs=(VMEM,) * n,
        compiler_params=pltpu.CompilerParams(vmem_limit_bytes=VMEM_LIMIT),
        cost_estimate=end_cost(n, span, cols),
    )(*masked, *pieces, *before)


def last_tiles(masked, jobs, first, outputs, block_total):
    cols, n = masked[0].shape[1], len(jobs)
    names, pieces, before, span, rows_of = split_jobs(jobs)
    n_in = len(pieces)

    def body(*refs):
        last_kernel(
            refs[:n], rows_of(refs[n:]), refs[n + n_in : 2 * n + n_in], *refs[2 * n + n_in + 2 :],
            names=names, first=first, block_total=block_total,
        )

    return pl.pallas_call(
        body,
        out_shape=tuple(jax.ShapeDtypeStruct(o.shape, o.dtype) for o in outputs),
        in_specs=[VMEM] * (2 * n + n_in) + [ANY] * 2,
        out_specs=(ANY,) * 2,
        scratch_shapes=[pltpu.VMEM((n, cols, cols), jnp.float32), pltpu.SemaphoreType.DMA((n,))],
        input_output_aliases={2 * n + n_in: 0, 2 * n + n_in + 1: 1},
        compiler_params=pltpu.CompilerParams(vmem_limit_bytes=VMEM_LIMIT),
        cost_estimate=end_cost(n, span, cols),
    )(*masked, *pieces, *before, *outputs)


def plan(total, head, turns, block_total, b_half, position, live_rows, significant):
    scalars = (position, live_rows, significant)

    def send(block, moves):
        return lax.ppermute(block, "ao", level_route(block_total, moves))

    cores = [(j, 0, j ^ 1) for j in range(LEVEL)]
    across = [(j, 0, j ^ 2) for j in range(LEVEL)]
    far = [(1, 1, 0), (0, -1, 1), (3, 1, 2), (2, -1, 3)]
    relay = [(0, 1, 0), (1, 1, 1), (2, -1, 2), (3, -1, 3)]
    turn = [(0, 1, 0), (3, -1, 3), (1, 0, 2), (2, 0, 1)]

    first = rows_after(b_half, 0, head)
    y_head = send(first, across)
    core = send(b_half, cores)
    later = rows_after(b_half, head, total - head, first, core)
    y_tail = send(later, across)
    far_head, far_tail = send(first, far), send(later, far)

    diagonal, own_t = own_tile(scalars, b_half, block_total)
    upper, lower, core_t, made_core = core_tile(scalars, core, own_t, block_total)
    turned = (own_t, core_t)
    y_head = after(y_head, made_core)
    relayed = send(y_head, relay)
    y_part, both_part, made_y = pair_tiles(scalars, turned, "across", [y_head], 0, head, None, None, block_total)
    both_part = send(both_part, cores)
    upper, lower, made_far = pair_tiles(
        scalars, turned, "far", [far_head, far_tail], 0, total, None, (upper, lower), block_total
    )

    masked = mask_rows(scalars, own_t, ("relay", "last"), head, block_total)
    y_tail = after(y_tail, made_y, made_far, masked[0])
    relay_tail = [send(piece, turn) for piece in pick(position, y_tail, far_tail, turns)]
    both_tail = send(y_tail, cores)
    relay_part, last_part, made_relay = pair_tiles(
        scalars, turned, "relay", [relayed], 0, head, None, None, block_total
    )
    last_part = send(last_part, cores)
    jobs = [("across", [y_tail], y_part), ("both", [both_tail], both_part)]
    upper, lower, made_across = end_tiles(scalars, own_t, jobs, head, (upper, lower), block_total)

    relay_tail[:2] = [after(piece, made_across, made_relay) for piece in relay_tail[:2]]
    last_tail = [send(piece, cores) for piece in relay_tail]
    jobs = [("relay", relay_tail[:-1], relay_part), ("last", last_tail[:-1], last_part)]
    relay_part, last_part = add_rows(masked, jobs)
    jobs = [("relay", relay_tail[-1:], relay_part), ("last", last_tail[-1:], last_part)]
    upper, lower = last_tiles(masked, jobs, sum(turns[:-1]), (upper, lower), block_total)
    return diagonal, upper, lower


def per_device(b_half, significant, live_rows):
    block_total = lax.axis_size("ao")
    position = lax.axis_index("ao").astype(jnp.int32)[None]
    steps = b_half.shape[0] // ROWBLK
    return plan(steps, 3, (1, 1, 1), block_total, b_half, position, live_rows, significant)


def solution(mesh):
    in_specs = (P("groups", "ao"), P("groups", None), P("groups"))
    out_specs = (
        P(("groups", "ao"), None, None),
        P(("groups", "ao"), None, None, None),
        P(("groups", "ao"), None, None, None),
    )
    return jax.shard_map(
        per_device, mesh=mesh, in_specs=in_specs, out_specs=out_specs, check_vma=False
    )
```

```python
import functools

import jax
import jax.numpy as jnp
from jax import lax
from jax.experimental import pallas as pl
from jax.experimental.pallas import tpu as pltpu
from jax.sharding import PartitionSpec as P

ROWBLK = 512
HOPS = 3
VMEM_LIMIT = 28 * 2**20
VMEM_ALL = 63 * 2**20
LEVEL = 4
PARTS = 4

SMEM = pl.BlockSpec(memory_space=pltpu.SMEM)
HBM = pl.BlockSpec(memory_space=pltpu.HBM)
ANY = pl.BlockSpec(memory_space=pl.ANY)
VMEM = pl.BlockSpec(memory_space=pltpu.VMEM)
TOKEN = jax.ShapeDtypeStruct((8, 128), jnp.float32)


def level_route(block_total, moves):
    levels = block_total // LEVEL
    return [
        (LEVEL * z + place, LEVEL * (z + step) + new)
        for z in range(levels)
        for place, step, new in moves
        if 0 <= z + step < levels
    ]


def start_tile(source, target, sem):
    rows = source.shape[0] // PARTS
    for part in range(PARTS):
        at = pl.ds(part * rows, rows)
        pltpu.make_async_copy(source.at[at], target.at[at], sem).start()


def wait_tile(tile, sem):
    pltpu.make_async_copy(tile, tile, sem).wait()


class Geometry:
    def __init__(self, position_ref, live_ref, sig_ref, block_total):
        self.live_ref, self.sig_ref, self.block_total = live_ref, sig_ref, block_total
        self.me = position_ref if live_ref is None else position_ref[0]
        self.place = lax.rem(self.me, LEVEL)
        even = lax.rem(self.place, 2) == 0
        self.upper = self.place >= 2
        self.edge = (self.place == 0) | (self.place == 3)
        self.core = self.me + jnp.where(even, 1, -1)
        self.across = self.me + jnp.where(self.upper, -2, 2)
        self.far = self.me + jnp.where(even, -3, 3)
        self.relay = self.me + jnp.where(self.upper, 2, -2)
        self.both = self.me + (LEVEL - 1) - 2 * self.place
        self.last = self.me + jnp.where(self.edge, 1, 3) * jnp.where(self.upper, 1, -1)

    def live(self, block):
        return self.live_ref[jnp.clip(block, 0, self.block_total - 1)] // ROWBLK

    def count(self, first, second):
        low = jnp.clip(jnp.minimum(first, second), 0, self.block_total - 1)
        hop = jnp.clip(jnp.abs(first - second) - 1, 0, HOPS - 1)
        inside = (second >= 0) & (second < self.block_total)
        rows = jnp.minimum(self.live(first), self.live(second))
        return jnp.where(inside, rows * self.sig_ref[low, hop], 0)

    def place_tile(self, tile, other, up_ref, low_ref, sem, enable=True):
        dist = other - self.me
        hop = jnp.clip(jnp.abs(dist) - 1, 0, HOPS - 1)

        @pl.when(enable & (dist > 0))
        def _():
            start_tile(tile, up_ref.at[0, hop], sem)

        @pl.when(enable & (dist < 0))
        def _():
            start_tile(tile, low_ref.at[0, hop], sem)


def rows_at(ref, r):
    return ref.at[pl.ds(r * ROWBLK, ROWBLK)]


def dot_into(total, left, right):
    total[...] += jnp.dot(left, right, preferred_element_type=jnp.float32)


def gate_kernel(*refs):
    del refs


def after(array, *tokens):
    return pl.pallas_call(
        gate_kernel,
        out_shape=jax.ShapeDtypeStruct(array.shape, array.dtype),
        in_specs=[ANY] * (1 + len(tokens)),
        out_specs=ANY,
        input_output_aliases={0: 0},
        compiler_params=pltpu.CompilerParams(vmem_limit_bytes=VMEM_LIMIT),
    )(array, *tokens)


def rows_kernel(block_ref, *refs, low):
    out_ref, held, in_sem, out_sem = refs[-4:]
    size = held.shape[0]
    part = held.shape[1]
    ins, outs = [], []
    for k in range(size):
        source, target = pl.ds(low * ROWBLK + k * part, part), pl.ds(k * part, part)
        ins.append(pltpu.make_async_copy(block_ref.at[source], held.at[k], in_sem.at[k]))
        outs.append(pltpu.make_async_copy(held.at[k], out_ref.at[target], out_sem.at[k]))
    for copy in ins:
        copy.start()
    for copy, out in zip(ins, outs):
        copy.wait()
        out.start()
    for out in outs:
        out.wait()


def rows_after(block, low, size, *tokens):
    cols = block.shape[1]
    return pl.pallas_call(
        functools.partial(rows_kernel, low=low),
        out_shape=jax.ShapeDtypeStruct((size * ROWBLK, cols), block.dtype),
        in_specs=[HBM] + [ANY] * len(tokens),
        out_specs=ANY,
        scratch_shapes=[
            pltpu.VMEM((4 * size, ROWBLK // 4, cols), block.dtype),
            pltpu.SemaphoreType.DMA((4 * size,)),
            pltpu.SemaphoreType.DMA((4 * size,)),
        ],
        compiler_params=pltpu.CompilerParams(vmem_limit_bytes=VMEM_ALL),
    )(block, *tokens)


def pick_kernel(position_ref, edge_ref, inner_ref, *refs, sizes):
    outs, (held, in_sem, out_sem) = refs[: len(sizes)], refs[len(sizes) :]
    place = lax.rem(position_ref[0], LEVEL)
    inner = (place == 1) | (place == 2)
    copies = []
    for out, at in [(out, at) for out, size in zip(outs, sizes) for at in range(size)]:
        k = len(copies)
        pl.when(inner)(pltpu.make_async_copy(rows_at(inner_ref, k), held.at[k], in_sem.at[k]).start)
        pl.when(jnp.logical_not(inner))(pltpu.make_async_copy(rows_at(edge_ref, k), held.at[k], in_sem.at[k]).start)
        copies.append(pltpu.make_async_copy(held.at[k], rows_at(out, at), out_sem.at[k]))
    for k, copy in enumerate(copies):
        pltpu.make_async_copy(rows_at(edge_ref, k), held.at[k], in_sem.at[k]).wait()
        copy.start()
    for copy in copies:
        copy.wait()


def pick(position, edge, inner, sizes):
    cols = edge.shape[1]
    total = sum(sizes)
    return pl.pallas_call(
        functools.partial(pick_kernel, sizes=sizes),
        out_shape=tuple(jax.ShapeDtypeStruct((size * ROWBLK, cols), edge.dtype) for size in sizes),
        in_specs=[SMEM] + [ANY] * 2,
        out_specs=(ANY,) * len(sizes),
        scratch_shapes=[
            pltpu.VMEM((total, ROWBLK, cols), edge.dtype),
            pltpu.SemaphoreType.DMA((total,)),
            pltpu.SemaphoreType.DMA((total,)),
        ],
        compiler_params=pltpu.CompilerParams(vmem_limit_bytes=VMEM_LIMIT),
    )(position, edge, inner)


def own_kernel(position_ref, live_ref, sig_ref, own_ref, diag_ref, own_t_ref, own, own_t, tile, in_sem, turned_sem, out_sem, *, block_total):
    steps = own.shape[0]
    geo = Geometry(position_ref, live_ref, sig_ref, block_total)
    count = geo.live(geo.me)

    def in_copy(r):
        return pltpu.make_async_copy(rows_at(own_ref, r), own.at[r], in_sem.at[r])

    def turned_copy(r):
        return pltpu.make_async_copy(own_t.at[r], own_t_ref.at[r], turned_sem.at[r])

    for r in range(steps):
        pl.when(r < count)(in_copy(r).start)
    tile[...] = jnp.zeros_like(tile)

    @pl.loop(0, count)
    def _(r):
        in_copy(r).wait()
        own_t[r] = own[r].T
        turned_copy(r).start()
        dot_into(tile, own_t[r], own[r])

    start_tile(tile, diag_ref.at[0], out_sem.at[0])

    @pl.loop(0, count)
    def _(r):
        turned_copy(r).wait()

    wait_tile(tile, out_sem.at[0])


def own_tile(scalars, own, block_total):
    rows, cols = own.shape
    steps = rows // ROWBLK
    return pl.pallas_call(
        functools.partial(own_kernel, block_total=block_total),
        out_shape=(
            jax.ShapeDtypeStruct((1, cols, cols), jnp.float32),
            jax.ShapeDtypeStruct((steps, cols, ROWBLK), own.dtype),
        ),
        in_specs=[SMEM] * 3 + [ANY],
        out_specs=(ANY,) * 2,
        scratch_shapes=[
            pltpu.VMEM((steps, ROWBLK, cols), own.dtype),
            pltpu.VMEM((steps, cols, ROWBLK), own.dtype),
            pltpu.VMEM((cols, cols), jnp.float32),
            pltpu.SemaphoreType.DMA((steps,)),
            pltpu.SemaphoreType.DMA((steps,)),
            pltpu.SemaphoreType.DMA((1,)),
        ],
        compiler_params=pltpu.CompilerParams(vmem_limit_bytes=VMEM_LIMIT),
        cost_estimate=pl.CostEstimate(
            flops=2 * rows * cols * cols, bytes_accessed=4 * rows * cols + 4 * cols * cols, transcendentals=0
        ),
    )(*scalars, own)


def core_kernel(
    position_ref, live_ref, sig_ref, core_ref, own_t_ref, up_ref, low_ref, core_t_ref, _token, own_t, core, core_t, tile, sems,
    turned_sem, out_sem, *, block_total,
):
    steps = core.shape[0]
    geo = Geometry(position_ref, live_ref, sig_ref, block_total)
    core_count = geo.live(geo.core)
    pair_count = geo.count(geo.me, geo.core)

    def core_copy(r):
        return pltpu.make_async_copy(rows_at(core_ref, r), core.at[r], sems.at[0, r])

    def own_copy(r):
        return pltpu.make_async_copy(own_t_ref.at[r], own_t.at[r], sems.at[1, r])

    def turned_copy(r):
        return pltpu.make_async_copy(core_t.at[r], core_t_ref.at[r], turned_sem.at[r])

    for r in range(steps):
        pl.when(r < core_count)(core_copy(r).start)
        pl.when(r < pair_count)(own_copy(r).start)
    tile[...] = jnp.zeros_like(tile)

    @pl.loop(0, core_count)
    def _(r):
        core_copy(r).wait()
        core_t[r] = core[r].T
        turned_copy(r).start()

        @pl.when(r < pair_count)
        def _():
            own_copy(r).wait()
            dot_into(tile, own_t[r], core[r])

    geo.place_tile(tile, geo.core, up_ref, low_ref, out_sem.at[0])

    @pl.loop(0, core_count)
    def _(r):
        turned_copy(r).wait()

    wait_tile(tile, out_sem.at[0])


def core_tile(scalars, core, own_t, block_total):
    rows, cols = core.shape
    steps = rows // ROWBLK
    three = jax.ShapeDtypeStruct((1, HOPS, cols, cols), jnp.float32)
    return pl.pallas_call(
        functools.partial(core_kernel, block_total=block_total),
        out_shape=(three, three, jax.ShapeDtypeStruct(own_t.shape, own_t.dtype), TOKEN),
        in_specs=[SMEM] * 3 + [ANY] * 2,
        out_specs=(ANY,) * 4,
        scratch_shapes=[
            pltpu.VMEM((steps, cols, ROWBLK), core.dtype),
            pltpu.VMEM((steps, ROWBLK, cols), core.dtype),
            pltpu.VMEM((steps, cols, ROWBLK), core.dtype),
            pltpu.VMEM((cols, cols), jnp.float32),
            pltpu.SemaphoreType.DMA((2, steps)),
            pltpu.SemaphoreType.DMA((steps,)),
            pltpu.SemaphoreType.DMA((1,)),
        ],
        compiler_params=pltpu.CompilerParams(vmem_limit_bytes=VMEM_LIMIT),
        cost_estimate=pl.CostEstimate(
            flops=2 * rows * cols * cols, bytes_accessed=6 * rows * cols + 4 * cols * cols, transcendentals=0
        ),
    )(*scalars, core, own_t)


def pair_kernel(
    position_ref, live_ref, sig_ref, own_t_ref, core_t_ref, piece_refs, before, outs, own_t, core_t, held, tiles, sems,
    before_sem, out_sem, *, which, low, high, sources, final, block_total,
):
    geo = Geometry(position_ref, live_ref, sig_ref, block_total)
    other = getattr(geo, which)
    shared = which != "far"
    count = geo.count(geo.me, other)
    core_count = geo.count(geo.core, other) if shared else 0
    either = jnp.maximum(count, core_count)

    for r in range(low, high):
        at, (ref, offset) = r - low, sources[r]
        own_copy = pltpu.make_async_copy(own_t_ref.at[r], own_t.at[at], sems.at[0, at])
        pl.when(r < count)(own_copy.start)
        if shared:
            core_copy = pltpu.make_async_copy(core_t_ref.at[r], core_t.at[at], sems.at[1, at])
            pl.when(r < core_count)(core_copy.start)
        held_copy = pltpu.make_async_copy(rows_at(piece_refs[ref], offset), held.at[at], sems.at[2, at])
        pl.when(r < either)(held_copy.start)

    if before:
        for i in range(2):
            start_tile(before[i], tiles.at[i], before_sem.at[i])
        for i in range(2):
            wait_tile(tiles.at[i], before_sem.at[i])
    else:
        tiles[...] = jnp.zeros_like(tiles)

    @pl.loop(0, high - low)
    def _(at):
        r = at + low

        @pl.when(r < either)
        def _():
            pltpu.make_async_copy(rows_at(piece_refs[0], 0), held.at[at], sems.at[2, at]).wait()

        @pl.when(r < count)
        def _():
            pltpu.make_async_copy(own_t_ref.at[0], own_t.at[at], sems.at[0, at]).wait()
            dot_into(tiles.at[0], own_t[at], held[at])

        if shared:
            @pl.when(r < core_count)
            def _():
                pltpu.make_async_copy(core_t_ref.at[0], core_t.at[at], sems.at[1, at]).wait()
                dot_into(tiles.at[1], core_t[at], held[at])

    if shared:
        start_tile(tiles.at[1], outs[-1], out_sem.at[1])
    if final:
        geo.place_tile(tiles.at[0], other, outs[0], outs[1], out_sem.at[0])
        wait_tile(tiles.at[0], out_sem.at[0])
    else:
        start_tile(tiles.at[0], outs[0], out_sem.at[0])
        wait_tile(tiles.at[0], out_sem.at[0])
    if shared:
        wait_tile(tiles.at[1], out_sem.at[1])


def pair_tiles(scalars, turned, which, pieces, low, high, before, outputs, block_total):
    steps, cols, _ = turned[0].shape
    tile = jax.ShapeDtypeStruct((cols, cols), jnp.float32)
    final = outputs is not None
    places = [(i, k) for i, piece in enumerate(pieces) for k in range(piece.shape[0] // ROWBLK)]
    sources = dict(zip(range(low, high), places))
    before, chained = list(before or ()), list(outputs or ())
    n_in, n_before = len(pieces), len(before)
    n_out = (2 if final else 1) + (which != "far")

    def body(position_ref, live_ref, sig_ref, own_t_ref, core_t_ref, *refs):
        outs_at = n_in + n_before + len(chained)
        pair_kernel(
            position_ref, live_ref, sig_ref, own_t_ref, core_t_ref, refs[:n_in], refs[n_in : n_in + n_before],
            refs[outs_at : outs_at + n_out], *refs[outs_at + n_out + 1 :],
            which=which, low=low, high=high, sources=sources, final=final, block_total=block_total,
        )

    span = high - low
    return pl.pallas_call(
        body,
        out_shape=tuple(jax.ShapeDtypeStruct(c.shape, c.dtype) for c in chained) + (tile,) * (n_out - len(chained)) + (TOKEN,),
        in_specs=[SMEM] * 3 + [ANY] * (2 + n_in + n_before + len(chained)),
        out_specs=(ANY,) * (n_out + 1),
        scratch_shapes=[pltpu.VMEM((span, cols, ROWBLK), turned[0].dtype)] * 2
        + [
            pltpu.VMEM((span, ROWBLK, cols), turned[0].dtype),
            pltpu.VMEM((2, cols, cols), jnp.float32),
            pltpu.SemaphoreType.DMA((3, span)),
            pltpu.SemaphoreType.DMA((2,)),
            pltpu.SemaphoreType.DMA((2,)),
        ],
        input_output_aliases={5 + n_in + n_before + i: i for i in range(len(chained))},
        compiler_params=pltpu.CompilerParams(vmem_limit_bytes=VMEM_LIMIT),
        cost_estimate=pl.CostEstimate(
            flops=4 * span * ROWBLK * cols * cols,
            bytes_accessed=6 * span * ROWBLK * cols + 16 * cols * cols,
            transcendentals=0,
        ),
    )(*scalars, *turned, *pieces, *before, *chained)


def end_kernel(
    position_ref, live_ref, sig_ref, own_t_ref, pieces, before, up_ref, low_ref, _token, tiles, out_sem, *, names, low,
    block_total,
):
    geo = Geometry(position_ref, live_ref, sig_ref, block_total)
    for i, name in enumerate(names):
        other = getattr(geo, name)
        count = geo.count(geo.me, other) - low
        tiles[i] = before[i][...]
        for at, rows in enumerate(pieces[i]):
            @pl.when(at < count)
            def _():
                dot_into(tiles.at[i], own_t_ref[low + at], rows[...])

        geo.place_tile(tiles.at[i], other, up_ref, low_ref, out_sem.at[i])
    for i in range(len(names)):
        wait_tile(tiles.at[i], out_sem.at[i])


def mask_kernel(position_ref, live_ref, sig_ref, own_t_ref, *masked, names, low, block_total):
    geo = Geometry(position_ref, live_ref, sig_ref, block_total)
    for out_ref, name in zip(masked, names):
        count = geo.count(geo.me, getattr(geo, name)) - low
        for k in range(out_ref.shape[0]):
            kept = own_t_ref[low + k]
            out_ref[k] = jnp.where(k < count, kept, jnp.zeros_like(kept))


def mask_rows(scalars, own_t, names, low, block_total):
    masked = jax.ShapeDtypeStruct((own_t.shape[0] - low, *own_t.shape[1:]), own_t.dtype)
    return pl.pallas_call(
        functools.partial(mask_kernel, names=names, low=low, block_total=block_total),
        out_shape=(masked,) * len(names),
        in_specs=[SMEM] * 3 + [VMEM],
        out_specs=(VMEM,) * len(names),
        compiler_params=pltpu.CompilerParams(vmem_limit_bytes=VMEM_LIMIT),
    )(*scalars, own_t)


def add_kernel(masked, ready, others, before, up_ref, low_ref, part_ref, tile, out_sem, *, names, block_total):
    geo = Geometry(lax.axis_index("ao"), None, None, block_total)
    for i, blocks in enumerate((ready, others)):
        total = before[i][...]
        for k, rows in enumerate(blocks):
            total += jnp.dot(masked[i][k], rows[...], preferred_element_type=jnp.float32)
        if i == 0:
            tile[...] = total
            geo.place_tile(tile, getattr(geo, names[0]), up_ref, low_ref, out_sem.at[0])
        else:
            part_ref[...] = total
    wait_tile(tile, out_sem.at[0])


def last_kernel(masked, pieces, before, up_ref, low_ref, tiles, out_sem, *, names, first, block_total):
    geo = Geometry(lax.axis_index("ao"), None, None, block_total)
    for i, name in enumerate(names):
        total = before[i][...]
        for k, rows in enumerate(pieces[i]):
            total += jnp.dot(masked[i][first + k], rows[...], preferred_element_type=jnp.float32)
        tiles[i] = total
        geo.place_tile(tiles.at[i], getattr(geo, name), up_ref, low_ref, out_sem.at[i])
    for i in range(len(names)):
        wait_tile(tiles.at[i], out_sem.at[i])


def split_jobs(jobs):
    pieces = [piece for job in jobs for piece in job[1]]
    places = [(p, k) for p, piece in enumerate(pieces) for k in range(piece.shape[0] // ROWBLK)]
    span = len(places) // len(jobs)

    def rows_of(refs):
        rows = [rows_at(refs[p], k) for p, k in places]
        return [rows[i * span : (i + 1) * span] for i in range(len(jobs))]

    return [job[0] for job in jobs], pieces, [job[2] for job in jobs], span, rows_of


def end_cost(n, span, cols):
    return pl.CostEstimate(
        flops=2 * n * span * ROWBLK * cols * cols,
        bytes_accessed=2 * (n + 1) * span * ROWBLK * cols + 8 * n * cols * cols,
        transcendentals=0,
    )


def end_tiles(scalars, own_t, jobs, low, outputs, block_total):
    cols, n = own_t.shape[1], len(jobs)
    names, pieces, before, span, rows_of = split_jobs(jobs)
    n_in = len(pieces)

    def body(position_ref, live_ref, sig_ref, own_t_ref, *refs):
        end_kernel(
            position_ref, live_ref, sig_ref, own_t_ref, rows_of(refs), refs[n_in : n_in + n], *refs[n_in + n + 2 :],
            names=names, low=low, block_total=block_total,
        )

    return pl.pallas_call(
        body,
        out_shape=(*(jax.ShapeDtypeStruct(o.shape, o.dtype) for o in outputs), TOKEN),
        in_specs=[SMEM] * 3 + [VMEM] * (1 + n_in + n) + [ANY] * 2,
        out_specs=(ANY,) * 3,
        scratch_shapes=[pltpu.VMEM((n, cols, cols), jnp.float32), pltpu.SemaphoreType.DMA((n,))],
        input_output_aliases={4 + n_in + n: 0, 5 + n_in + n: 1},
        compiler_params=pltpu.CompilerParams(vmem_limit_bytes=VMEM_LIMIT),
        cost_estimate=end_cost(n, span, cols),
    )(*scalars, own_t, *pieces, *before, *outputs)


def add_rows(masked, jobs, outputs, block_total):
    cols = masked[0].shape[1]
    names = [job[0] for job in jobs]
    pieces = [list(job[1]) for job in jobs]
    before = [job[2] for job in jobs]
    arrays = [*pieces[0], *pieces[1]]
    n, n_first = len(arrays), len(pieces[0])

    def body(*refs):
        blocks = [[rows_at(ref, k) for ref in refs[low:high] for k in range(ref.shape[0] // ROWBLK)]
                  for low, high in ((2, 2 + n_first), (2 + n_first, 2 + n))]
        add_kernel(
            refs[:2], *blocks, refs[2 + n : 4 + n], *refs[6 + n :], names=names, block_total=block_total,
        )

    return pl.pallas_call(
        body,
        out_shape=(
            *(jax.ShapeDtypeStruct(o.shape, o.dtype) for o in outputs),
            jax.ShapeDtypeStruct(before[1].shape, jnp.float32),
        ),
        in_specs=[VMEM] * (4 + n) + [ANY] * 2,
        out_specs=(ANY, ANY, VMEM),
        scratch_shapes=[pltpu.VMEM((cols, cols), jnp.float32), pltpu.SemaphoreType.DMA((1,))],
        input_output_aliases={4 + n: 0, 5 + n: 1},
        compiler_params=pltpu.CompilerParams(vmem_limit_bytes=VMEM_LIMIT),
        cost_estimate=end_cost(2, 2, cols),
    )(*masked, *arrays, *before, *outputs)


def last_tiles(masked, jobs, first, outputs, block_total):
    cols, n = masked[0].shape[1], len(jobs)
    names, pieces, before, span, rows_of = split_jobs(jobs)
    n_in = len(pieces)

    def body(*refs):
        last_kernel(
            refs[:n], rows_of(refs[n:]), refs[n + n_in : 2 * n + n_in], *refs[2 * n + n_in + 2 :],
            names=names, first=first, block_total=block_total,
        )

    return pl.pallas_call(
        body,
        out_shape=tuple(jax.ShapeDtypeStruct(o.shape, o.dtype) for o in outputs),
        in_specs=[VMEM] * (2 * n + n_in) + [ANY] * 2,
        out_specs=(ANY,) * 2,
        scratch_shapes=[pltpu.VMEM((n, cols, cols), jnp.float32), pltpu.SemaphoreType.DMA((n,))],
        input_output_aliases={2 * n + n_in: 0, 2 * n + n_in + 1: 1},
        compiler_params=pltpu.CompilerParams(vmem_limit_bytes=VMEM_LIMIT),
        cost_estimate=end_cost(n, span, cols),
    )(*masked, *pieces, *before, *outputs)


def plan(total, head, turns, block_total, b_half, position, live_rows, significant):
    scalars = (position, live_rows, significant)

    def send(block, moves):
        return lax.ppermute(block, "ao", level_route(block_total, moves))

    cores = [(j, 0, j ^ 1) for j in range(LEVEL)]
    across = [(j, 0, j ^ 2) for j in range(LEVEL)]
    far = [(1, 1, 0), (0, -1, 1), (3, 1, 2), (2, -1, 3)]
    relay = [(0, 1, 0), (1, 1, 1), (2, -1, 2), (3, -1, 3)]
    turn = [(0, 1, 0), (3, -1, 3), (1, 0, 2), (2, 0, 1)]

    first = rows_after(b_half, 0, head)
    y_head = send(first, across)
    core = send(b_half, cores)
    later = rows_after(b_half, head, total - head, first, core)
    y_tail = send(later, across)
    far_head, far_tail = send(first, far), send(later, far)

    diagonal, own_t = own_tile(scalars, b_half, block_total)
    upper, lower, core_t, made_core = core_tile(scalars, core, own_t, block_total)
    turned = (own_t, core_t)
    y_head = after(y_head, made_core)
    relayed = send(y_head, relay)
    y_part, both_part, made_y = pair_tiles(scalars, turned, "across", [y_head], 0, head, None, None, block_total)
    both_part = send(both_part, cores)
    upper, lower, made_far = pair_tiles(
        scalars, turned, "far", [far_head, far_tail], 0, total, None, (upper, lower), block_total
    )

    masked = mask_rows(scalars, own_t, ("relay", "last"), head, block_total)
    y_tail = after(y_tail, made_y, made_far, masked[0])
    relay_tail = [send(piece, turn) for piece in pick(position, y_tail, far_tail, turns)]
    both_tail = send(y_tail, cores)
    relay_part, last_part, made_relay = pair_tiles(
        scalars, turned, "relay", [relayed], 0, head, None, None, block_total
    )
    last_part = send(last_part, cores)
    jobs = [("across", [y_tail], y_part), ("both", [both_tail], both_part)]
    upper, lower, made_across = end_tiles(scalars, own_t, jobs, head, (upper, lower), block_total)

    relay_tail[:2] = [after(piece, made_across, made_relay) for piece in relay_tail[:2]]
    last_tail = [send(piece, cores) for piece in relay_tail]
    jobs = [("relay", relay_tail, relay_part), ("last", last_tail[:-1], last_part)]
    upper, lower, last_part = add_rows(masked, jobs, (upper, lower), block_total)
    jobs = [("last", last_tail[-1:], last_part)]
    upper, lower = last_tiles(masked[1:], jobs, sum(turns[:-1]), (upper, lower), block_total)
    return diagonal, upper, lower


def per_device(b_half, significant, live_rows):
    block_total = lax.axis_size("ao")
    position = lax.axis_index("ao").astype(jnp.int32)[None]
    steps = b_half.shape[0] // ROWBLK
    return plan(steps, 3, (1, 1, 1), block_total, b_half, position, live_rows, significant)


def solution(mesh):
    in_specs = (P("groups", "ao"), P("groups", None), P("groups"))
    out_specs = (
        P(("groups", "ao"), None, None),
        P(("groups", "ao"), None, None, None),
        P(("groups", "ao"), None, None, None),
    )
    return jax.shard_map(
        per_device, mesh=mesh, in_specs=in_specs, out_specs=out_specs, check_vma=False
    )
```
